512 devices in a mesh: rep: 16 (over z), fsdp: 32 (over x, y, core).
Axes of the slice: x: 4, y: 4, z: 16, core: 2. Of those that a mesh axis runs over, the one named last changes fastest.
Arguments:
- gradient: bfloat16 [128, 1024, 1024], P(None, 'fsdp', 'rep')
- owner_slot: int32 [128], replicated, may hold values from 0 to 127, each once
- left_factor: bfloat16 [131072, 1024], P(('rep', 'fsdp'))
- right_factor: bfloat16 [131072, 1024], P(('rep', 'fsdp'))
- left_root: bfloat16 [131072, 1024], P(('rep', 'fsdp'))
- right_root: bfloat16 [131072, 1024], P(('rep', 'fsdp'))
Outputs:
- direction: bfloat16 [128, 1024, 1024], P(None, 'fsdp', 'rep')
- left_new: bfloat16 [131072, 1024], P(('rep', 'fsdp'))
- right_new: bfloat16 [131072, 1024], P(('rep', 'fsdp'))
The draws below stay inside these ranges and needn't reach their ends.
Inputs may be any that keep to these rules, and one draw needn't show every extreme that they name: owner_slot names every slot of 0 to 127 exactly once.
All inputs are finite; a program needn't handle non-finite values.
Results may differ from the reference program's by a relative error of at most 0.0057.
Values may be sent and summed in bfloat16 or wider, within the bound.
A program may use at most 64 MiB of HBM per device.

```python
import math
import jax
import jax.numpy as jnp
from jax import lax

B = 1024
NBLK = 128


def block_identity():
    row_pos = jnp.arange(NBLK * B, dtype=jnp.int32) % B
    columns = jnp.arange(B, dtype=jnp.int32)
    return (row_pos[:, None] == columns[None, :]).astype(jnp.float32)


def draw_gradient(key, part):
    key = jax.random.fold_in(key, 7)
    base_key, row_key, col_key = jax.random.split(key, 3)
    row_scale = jnp.exp(jax.random.uniform(row_key, (NBLK, B, 1), jnp.float32, -0.7, 0.7))
    col_scale = jnp.exp(jax.random.uniform(col_key, (NBLK, 1, B), jnp.float32, -0.7, 0.7))
    position = jnp.arange(B, dtype=jnp.float32) / B
    base = jnp.clip(jax.random.normal(base_key, (NBLK, B, B), jnp.float32), -4.0, 4.0)
    rising = 2.0
    values = 0.25 * base * row_scale * col_scale
    values = values * (1.0 + rising * position)[None, :, None] * (1.0 + rising * position)[None, None, :]
    return values.astype(jnp.bfloat16)


def slot_column(key, low, high):
    values = jax.random.uniform(key, (NBLK,), jnp.float32, low, high)
    return jnp.repeat(values, B)[:, None]


def scaled_factor(key, noise):
    slot_scale = jnp.exp(slot_column(key, math.log(0.5), math.log(2.0)))
    return (slot_scale * (block_identity() + 0.5 / math.sqrt(B) * noise)).astype(jnp.bfloat16)


def shaped_root(key, noise, rising):
    rough_key, scale_key, amp_key = jax.random.split(key, 3)
    position = (jnp.arange(NBLK * B, dtype=jnp.int32) % B).astype(jnp.float32) / B
    rough = jnp.exp(jax.random.uniform(rough_key, (NBLK * B,), jnp.float32, -0.3, 0.3))
    diag_values = (1.0 + rising * position) ** (-0.5) * rough
    slot_scale = jnp.exp(slot_column(scale_key, math.log(0.5), math.log(2.0)))
    amplitude = slot_column(amp_key, 0.2, 0.5)
    values = slot_scale * (block_identity() * diag_values[:, None] + amplitude / math.sqrt(B) * noise)
    return values.astype(jnp.bfloat16)


def draw_left_factor(key, part):
    key = jax.random.fold_in(key, 11)
    noise_key, scale_key = jax.random.split(key)
    noise = jax.random.normal(noise_key, (NBLK * B, B), jnp.float32)
    return scaled_factor(scale_key, noise)


def draw_right_factor(key, part):
    key = jax.random.fold_in(key, 13)
    noise_key, scale_key = jax.random.split(key)
    noise = jax.random.normal(noise_key, (NBLK * B, B), jnp.float32)
    return scaled_factor(scale_key, noise)


def draw_left_root(key, part):
    key = jax.random.fold_in(key, 17)
    noise_key, shape_key = jax.random.split(key)
    noise = jax.random.normal(noise_key, (NBLK * B, B), jnp.float32)
    rising = 2.0
    return shaped_root(shape_key, noise, rising)


def draw_right_root(key, part):
    key = jax.random.fold_in(key, 19)
    noise_key, shape_key = jax.random.split(key)
    noise = jax.random.normal(noise_key, (NBLK * B, B), jnp.float32)
    rising = 2.0
    return shaped_root(shape_key, noise, rising)


def setup_inputs(seed: int = 0) -> dict:
    splits = jax.random.split(jax.random.key(seed), 7)
    return {
        "gradient": draw_gradient(jax.random.fold_in(splits[6], 71), 0),
        "owner_slot": jax.random.permutation(splits[1], NBLK).astype(jnp.int32),
        "left_factor": draw_left_factor(jax.random.fold_in(splits[6], 71), 0),
        "right_factor": draw_right_factor(jax.random.fold_in(splits[6], 71), 0),
        "left_root": draw_left_root(jax.random.fold_in(splits[6], 71), 0),
        "right_root": draw_right_root(jax.random.fold_in(splits[6], 71), 0),
    }


BETA = 0.9
EPS = 1e-06

def reference(gradient, owner_slot, left_factor, right_factor, left_root, right_root):
    slot_ids = jnp.arange(NBLK, dtype=jnp.int32)
    matches = (owner_slot[:, None] == slot_ids[None, :]).astype(jnp.int32)
    inverse = lax.optimization_barrier(jnp.sum(matches * slot_ids[:, None], axis=0)).astype(jnp.int32)
    left_blocks = left_factor.reshape(NBLK, B, B)
    right_blocks = right_factor.reshape(NBLK, B, B)
    left_roots = left_root.reshape(NBLK, B, B)
    right_roots = right_root.reshape(NBLK, B, B)

    def per_slot(slot):
        grad_block = lax.dynamic_index_in_dim(gradient, inverse[slot], 0, keepdims=False)
        left_old = lax.dynamic_index_in_dim(left_blocks, slot, 0, keepdims=False)
        right_old = lax.dynamic_index_in_dim(right_blocks, slot, 0, keepdims=False)
        left_inv = lax.dynamic_index_in_dim(left_roots, slot, 0, keepdims=False)
        right_inv = lax.dynamic_index_in_dim(right_roots, slot, 0, keepdims=False)
        gram_left = lax.dot_general(grad_block, grad_block, (((1,), (1,)), ((), ())), preferred_element_type=jnp.float32)
        updated_left = (BETA * left_old.astype(jnp.float32) + (1.0 - BETA) / B * gram_left).astype(jnp.bfloat16)
        gram_right = lax.dot_general(grad_block, grad_block, (((0,), (0,)), ((), ())), preferred_element_type=jnp.float32)
        updated_right = (BETA * right_old.astype(jnp.float32) + (1.0 - BETA) / B * gram_right).astype(jnp.bfloat16)
        right_half = lax.dot_general(grad_block, right_inv, (((1,), (1,)), ((), ())), preferred_element_type=jnp.float32).astype(jnp.bfloat16)
        precond = jnp.dot(left_inv, right_half, preferred_element_type=jnp.float32).astype(jnp.bfloat16)
        prec_sq = jnp.sum(precond.astype(jnp.float32) ** 2)
        grad_sq = jnp.sum(grad_block.astype(jnp.float32) ** 2)
        return (updated_left, updated_right, precond, prec_sq, grad_sq)
    updated_left, updated_right, precond, prec_sq, grad_sq = lax.map(per_slot, slot_ids)
    per_block = jnp.take(precond, owner_slot, axis=0)
    prec_block = jnp.take(prec_sq, owner_slot, axis=0)
    grad_block_sq = jnp.take(grad_sq, owner_slot, axis=0)
    ratio = jnp.sqrt((grad_block_sq + EPS) / (prec_block + EPS))
    direction = (per_block.astype(jnp.float32) * ratio[:, None, None]).astype(jnp.bfloat16)
    return (direction, updated_left.reshape(NBLK * B, B), updated_right.reshape(NBLK * B, B))
```

```python
import functools

import jax
import jax.numpy as jnp
from jax import lax
from jax.experimental import pallas as pl
from jax.experimental.pallas import tpu as pltpu
from jax.sharding import PartitionSpec as P

MESH = pl.DeviceIdType.MESH
F32 = jnp.float32
BF16 = jnp.bfloat16
B = 1024
GROUP = 4
BETA = 0.9
EPS = 1e-06
NZ = 16
NF = 32
NQ = NF // GROUP
QUARTER = B // GROUP
LANES = 128
NT = (((1,), (1,)), ((), ()))
TN = (((0,), (0,)), ((), ()))
STEPS = (1, -1, 2, -2, 3, -3, 4, -4, 5, -5, 6, -6, 7, -7, 8)


def halves(even, odd):
    lane = lax.broadcasted_iota(jnp.int32, even.shape, even.ndim - 1)
    low = lane < LANES // 2
    axis = even.ndim - 1
    top = jnp.where(low, even, pltpu.roll(odd, LANES // 2, axis))
    bottom = jnp.where(low, pltpu.roll(even, LANES // 2, axis), odd)
    return top, bottom


def kernel(
    owner_ref, grad_in, lf_in, rf_in, lr_in, rr_in,
    final, ln_out, rn_out,
    grad, wide, send_fwd, mid_fwd, raw, block, lroot, rroot, lfac, rfac,
    tpart, acc, pre, sums, send_back, mid_back, lnew, rnew,
    in_sem, out_sem, zf_s, zf_r, xf_s, xf_r, sib_s, sib_r, r_s, r_r,
    ex_s, ex_r, zb_s, zb_r, xb_s, xb_r,
):
    z = lax.axis_index("rep")
    f = lax.axis_index("fsdp")
    core = f % 2
    xy = f // 2
    m = f % GROUP
    own_q = f // GROUP
    x = f // 8
    zq = z // 4
    sibling = f + 1 - 2 * core
    across = f + 2 - 4 * (m // 2)
    m_across = m + 2 - 4 * (m // 2)
    near = 1 + 2 * (1 - (z % 4) // 2)
    quads = [zq, (zq + near) % 4, (zq + 4 - near) % 4, (zq + 2) % 4]

    def local(src, dst, sem):
        return pltpu.make_async_copy(src, dst, sem)

    def remote(src, dst, send, recv, zd, fd):
        return pltpu.make_async_remote_copy(
            src_ref=src, dst_ref=dst, send_sem=send, recv_sem=recv,
            device_id=(zd, fd), device_id_type=MESH,
        )

    def await_bytes(ref, sem):
        pltpu.make_async_copy(ref, ref, sem).wait()

    loads = [
        local(grad_in, grad, in_sem.at[0]),
        local(lr_in, lroot, in_sem.at[1]),
        local(rr_in, rroot.at[m], in_sem.at[2]),
        local(lf_in, lfac, in_sem.at[3]),
        local(rf_in, rfac, in_sem.at[4]),
    ]
    for load in loads:
        load.start()
    barrier = pltpu.get_barrier_semaphore()

    def greet_plane(i, carry):
        pl.semaphore_signal(barrier, inc=1, device_id=(z, (f + i) % NF), device_id_type=MESH)
        return carry

    def greet_ring(i, carry):
        pl.semaphore_signal(barrier, inc=1, device_id=((z + i) % NZ, f), device_id_type=MESH)
        return carry

    lax.fori_loop(1, NZ, greet_ring, 0)
    lax.fori_loop(1, NF, greet_plane, 0)

    owner = owner_ref[...]
    slot_row = lax.broadcasted_iota(jnp.int32, (LANES, LANES), 0)
    pick = (jnp.broadcast_to(owner, (LANES, LANES)) == slot_row).astype(BF16)
    loads[0].wait()
    for t in range(16):
        piece = jnp.concatenate((grad[t * 64 : t * 64 + 64, :], grad[(16 + t) * 64 : (16 + t) * 64 + 64, :]), axis=0)
        wide[pl.ds(t, LANES, stride=16), :] = lax.dot_general(pick, piece, NT, preferred_element_type=F32)
    for zd in range(NZ):
        send_fwd[zd] = wide[zd * 128 : zd * 128 + 128, :].reshape(NQ, 16, LANES).astype(BF16)

    pl.semaphore_wait(barrier, NZ - 1 + NF - 1)

    def send_z(zd):
        remote(send_fwd.at[zd], mid_fwd.at[z], zf_s, zf_r.at[z], zd, f).start()

    for step in STEPS:
        send_z((z + step + NZ) % NZ)
    local(send_fwd.at[z], mid_fwd.at[z], zf_r.at[z]).start()

    remote(rr_in, rroot.at[m], r_s.at[0], r_r.at[0], z, across).start()
    remote(rr_in, rroot.at[m], r_s.at[1], r_r.at[1], z, sibling).start()

    def forward_xy(qd):
        for t in range(4):
            await_bytes(mid_fwd.at[qd * 4 + t], zf_r.at[qd * 4 + t])

        def one(i, carry):
            q, chip = i // 2, i % 2
            fd = q * GROUP + chip * 2 + core
            src = mid_fwd.at[pl.ds(qd * 4, 4), q]
            dst = raw.at[xy, core, pl.ds(qd * 4, 4)]

            @pl.when(fd != f)
            def _():
                remote(src, dst, xf_s.at[qd], xf_r.at[qd], z, fd).start()

            @pl.when(fd == f)
            def _():
                local(src, dst, xf_r.at[qd]).start()

            return carry

        lax.fori_loop(0, 2 * NQ, one, 0)

    def share(qd):
        mine = raw.at[:, core, pl.ds(qd * 4, 4)]
        await_bytes(mine, xf_r.at[qd])
        remote(mine, mine, sib_s.at[qd], sib_r.at[qd], z, sibling).start()

    def gather_chunk(qd):
        await_bytes(raw.at[:, 1 - core, pl.ds(qd * 4, 4)], sib_r.at[qd])

        def unpack(i, carry):
            for pair in range(2):
                first = qd * 4 + 2 * pair
                even = raw[pl.ds(i * 2, 2), :, first].reshape(64, LANES)
                odd = raw[pl.ds(i * 2, 2), :, first + 1].reshape(64, LANES)
                top, bottom = halves(even, odd)
                rows = jnp.concatenate((top.reshape(4, 16, LANES), bottom.reshape(4, 16, LANES)), axis=1)
                at = pl.multiple_of(i * 128, 128)
                block[qd, pl.ds(at, 128), pair * LANES : (pair + 1) * LANES] = rows.reshape(128, LANES)
            return carry

        lax.fori_loop(0, NF // 4, unpack, 0)

    def left_product(qd):
        tpart[qd] = jnp.dot(lroot[...], block[qd], preferred_element_type=F32).astype(BF16)

    def right_product(qd, first=False, last=False):
        squares = jnp.zeros((8, LANES), F32)
        for j in range(GROUP):
            cols = slice(j * QUARTER, (j + 1) * QUARTER)
            part = lax.dot_general(
                tpart[qd], rroot[j, :, pl.ds(pl.multiple_of(qd * QUARTER, QUARTER), QUARTER)], NT,
                preferred_element_type=F32,
            )
            if first:
                acc[:, cols] = part
            elif not last:
                acc[:, cols] += part
            else:
                value = (acc[:, cols] + part).astype(BF16)
                pre[:, cols] = value
                wider = value.astype(F32)
                squares += jnp.sum((wider * wider).reshape(QUARTER // 8, 8, 2, LANES), axis=(0, 2))
        return squares

    def grad_squares(qd, total):
        rows = block[qd, pl.ds(pl.multiple_of(m * QUARTER, QUARTER), QUARTER), :].astype(F32)
        return total + jnp.sum((rows * rows).reshape(QUARTER // 8, 8, 2, LANES), axis=(0, 2))

    total = jnp.zeros((8, LANES), F32)
    forward_xy(quads[0])
    forward_xy(quads[1])
    loads[1].wait()
    share(quads[0])
    forward_xy(quads[2])
    share(quads[1])
    gather_chunk(quads[0])
    left_product(quads[0])
    total = grad_squares(quads[0], total)
    forward_xy(quads[3])
    await_bytes(rroot.at[m_across], r_r.at[0])
    remote(rroot.at[m_across], rroot.at[m_across], r_s.at[2], r_r.at[2], z, sibling).start()
    share(quads[2])
    gather_chunk(quads[1])
    left_product(quads[1])
    total = grad_squares(quads[1], total)
    loads[2].wait()
    await_bytes(rroot.at[0], r_r.at[1])
    await_bytes(rroot.at[0], r_r.at[2])
    right_product(quads[0], first=True)
    right_product(quads[1])
    share(quads[3])
    gather_chunk(quads[2])
    left_product(quads[2])
    total = grad_squares(quads[2], total)
    right_product(quads[2])
    gather_chunk(quads[3])
    left_product(quads[3])
    prec_total = right_product(quads[3], last=True)
    total = grad_squares(quads[3], total)

    sums[m, 0] = total
    sums[m, 1] = prec_total
    for step in range(1, GROUP):
        fd = own_q * GROUP + (m + step) % GROUP
        remote(sums.at[m], sums.at[m], ex_s.at[step - 1], ex_r.at[m], z, fd).start()
    for step in range(1, GROUP):
        await_bytes(sums.at[0], ex_r.at[(m + step) % GROUP])
    grad_sq = jnp.sum(sums[0, 0] + sums[1, 0] + sums[2, 0] + sums[3, 0], keepdims=True)
    prec_sq = jnp.sum(sums[0, 1] + sums[1, 1] + sums[2, 1] + sums[3, 1], keepdims=True)
    ratio = jnp.sqrt((grad_sq + EPS) / (prec_sq + EPS))

    def pack_quad(qd):
        for pair in range(2):
            col = pl.multiple_of(qd * QUARTER + pair * LANES, LANES)
            rows = (pre[:, pl.ds(col, LANES)].astype(F32) * ratio).astype(BF16).reshape(NQ, 2, 16, LANES)
            even, odd = halves(rows[:, 0].reshape(LANES, LANES), rows[:, 1].reshape(LANES, LANES))
            send_back[qd * 4 + 2 * pair] = even.reshape(NQ, 16, LANES)
            send_back[qd * 4 + 2 * pair + 1] = odd.reshape(NQ, 16, LANES)

    def send_z_back(zd):
        remote(send_back.at[zd], mid_back.at[z], zb_s, zb_r.at[z], zd, f).start()

    for qd in quads:
        pack_quad(qd)
    for step in STEPS:
        send_z_back((z + step + NZ) % NZ)
    local(send_back.at[z], mid_back.at[z], zb_r.at[z]).start()

    def back_xy(qd):
        for t in range(4):
            await_bytes(mid_back.at[qd * 4 + t], zb_r.at[qd * 4 + t])

        def one(d, carry):
            fd = m * NQ + d
            src = mid_back.at[pl.ds(qd * 4, 4), d]
            dst = final.at[own_q, pl.ds(qd * 4, 4)]

            @pl.when(fd != f)
            def _():
                remote(src, dst, xb_s.at[qd], xb_r.at[qd], z, fd).start()

            @pl.when(fd == f)
            def _():
                local(src, dst, xb_r.at[qd]).start()

            return carry

        lax.fori_loop(0, NQ, one, 0)

    def gram_left():
        rows = pl.ds(pl.multiple_of(m * QUARTER, QUARTER), QUARTER)
        for j in range(GROUP):
            gram = jnp.zeros((QUARTER, QUARTER), F32)
            for c in range(4):
                gram += lax.dot_general(
                    block[c, rows, :], block[c, j * QUARTER : (j + 1) * QUARTER, :], NT, preferred_element_type=F32
                )
            cols = slice(j * QUARTER, (j + 1) * QUARTER)
            lnew[:, cols] = (BETA * lfac[:, cols].astype(F32) + (1.0 - BETA) / B * gram).astype(BF16)

    def gram_right():
        for j in range(GROUP):
            gram = lax.dot_general(block[m], block[j], TN, preferred_element_type=F32)
            cols = slice(j * QUARTER, (j + 1) * QUARTER)
            rnew[:, cols] = (BETA * rfac[:, cols].astype(F32) + (1.0 - BETA) / B * gram).astype(BF16)

    loads[3].wait()
    gram_left()
    stores = [local(lnew, ln_out, out_sem.at[0]), local(rnew, rn_out, out_sem.at[1])]
    stores[0].start()
    back_xy(quads[0])
    loads[4].wait()
    gram_right()
    stores[1].start()
    back_xy(quads[1])
    back_xy(quads[2])
    back_xy(quads[3])

    for qd in quads:
        await_bytes(final.at[:, pl.ds(qd * 4, 4)], xb_r.at[qd])

    await_bytes(send_fwd.at[pl.ds(0, NZ - 1)], zf_s)
    await_bytes(send_back.at[pl.ds(0, NZ - 1)], zb_s)
    for c in range(4):
        await_bytes(raw.at[pl.ds(0, 15), 0, pl.ds(0, 4)], xf_s.at[c])
        await_bytes(raw.at[:, 0, pl.ds(0, 4)], sib_s.at[c])

        @pl.when(x == m)
        def _():
            await_bytes(final.at[pl.ds(0, NQ - 1), pl.ds(0, 4)], xb_s.at[c])

        @pl.when(x != m)
        def _():
            await_bytes(final.at[:, pl.ds(0, 4)], xb_s.at[c])

    for i in range(3):
        await_bytes(rroot.at[0], r_s.at[i])
        await_bytes(sums.at[0], ex_s.at[i])
    stores[0].wait()
    stores[1].wait()


def finish(owner_ref, final, lnew, rnew, dir_out, ln_out, rn_out, rows_in, wide, dirv, lvmem, rvmem, in_sem, out_sem):
    loads = [pltpu.make_async_copy(final.at[q], rows_in.at[q], in_sem.at[q]) for q in range(NQ)]
    stores = [
        pltpu.make_async_copy(lvmem, ln_out, out_sem.at[0]),
        pltpu.make_async_copy(rvmem, rn_out, out_sem.at[1]),
        pltpu.make_async_copy(dirv, dir_out, out_sem.at[2]),
    ]
    loads.append(pltpu.make_async_copy(lnew, lvmem, in_sem.at[NQ]))
    loads.append(pltpu.make_async_copy(rnew, rvmem, in_sem.at[NQ + 1]))
    for copy in loads:
        copy.start()
    row = lax.broadcasted_iota(jnp.int32, (LANES, LANES), 0)
    slot_of = (row % NZ) * NQ + row // NZ
    place = (jnp.broadcast_to(owner_ref[...], (LANES, LANES)) == slot_of).astype(BF16)
    for q in range(NQ):
        loads[q].wait()
        wide[q * 256 : q * 256 + 256, :] = rows_in[q].reshape(256, LANES).astype(F32)
    for i in range(2):
        loads[NQ + i].wait()
        stores[i].start()
    for t in range(16):
        rows = wide[pl.ds(t, LANES, stride=16), :].astype(BF16)
        blocks = lax.dot_general(rows, place, TN, preferred_element_type=F32).astype(BF16)
        dirv[t * 64 : t * 64 + 64, :] = blocks[:64]
        dirv[(16 + t) * 64 : (16 + t) * 64 + 64, :] = blocks[64:]
    stores[2].start()
    for copy in stores:
        copy.wait()


def per_device(gradient, owner_slot, left_factor, right_factor, left_root, right_root):
    blocks, row_width, col_width = gradient.shape
    columns = gradient.transpose(1, 2, 0).reshape(row_width * col_width, blocks)
    anywhere = pl.BlockSpec(memory_space=pl.ANY)
    factor = jax.ShapeDtypeStruct((QUARTER, B), BF16)
    dma = pltpu.SemaphoreType.DMA
    owner = owner_slot.reshape(1, blocks)
    final, left_new, right_new = pl.pallas_call(
        kernel,
        out_shape=(jax.ShapeDtypeStruct((NQ, NZ, 16, LANES), BF16), factor, factor),
        in_specs=[pl.BlockSpec(memory_space=pltpu.VMEM)] + [anywhere] * 5,
        out_specs=(anywhere, anywhere, anywhere),
        scratch_shapes=[
            pltpu.VMEM((2048, LANES), BF16),
            pltpu.VMEM((2048, LANES), F32),
            pltpu.VMEM((NZ, NQ, 16, LANES), BF16),
            pltpu.VMEM((NZ, NQ, 16, LANES), BF16),
            pltpu.VMEM((NF // 2, 2, NZ, 16, LANES), BF16),
            pltpu.VMEM((4, B, QUARTER), BF16),
            pltpu.VMEM((QUARTER, B), BF16),
            pltpu.VMEM((GROUP, QUARTER, B), BF16),
            pltpu.VMEM((QUARTER, B), BF16),
            pltpu.VMEM((QUARTER, B), BF16),
            pltpu.VMEM((4, QUARTER, QUARTER), BF16),
            pltpu.VMEM((QUARTER, B), F32),
            pltpu.VMEM((QUARTER, B), BF16),
            pltpu.VMEM((GROUP, 2, 8, LANES), F32),
            pltpu.VMEM((NZ, NQ, 16, LANES), BF16),
            pltpu.VMEM((NZ, NQ, 16, LANES), BF16),
            pltpu.VMEM((QUARTER, B), BF16),
            pltpu.VMEM((QUARTER, B), BF16),
            dma((5,)), dma((2,)),
            dma, dma((NZ,)),
            dma((4,)), dma((4,)),
            dma((4,)), dma((4,)),
            dma((3,)), dma((3,)),
            dma((3,)), dma((GROUP,)),
            dma, dma((NZ,)),
            dma((4,)), dma((4,)),
        ],
        compiler_params=pltpu.CompilerParams(
            collective_id=0, has_side_effects=True, vmem_limit_bytes=60 * 1024 * 1024
        ),
        cost_estimate=pl.CostEstimate(flops=2_200_000_000, bytes_accessed=8_000_000, transcendentals=0),
    )(owner, columns, left_factor, right_factor, left_root, right_root)
    direction, left_new, right_new = pl.pallas_call(
        finish,
        out_shape=(jax.ShapeDtypeStruct(columns.shape, BF16), factor, factor),
        in_specs=[pl.BlockSpec(memory_space=pltpu.VMEM)] + [anywhere] * 3,
        out_specs=(anywhere, anywhere, anywhere),
        scratch_shapes=[
            pltpu.VMEM((NQ, NZ, 16, LANES), BF16),
            pltpu.VMEM((2048, LANES), F32),
            pltpu.VMEM((2048, LANES), BF16),
            pltpu.VMEM((QUARTER, B), BF16),
            pltpu.VMEM((QUARTER, B), BF16),
            dma((NQ + 2,)),
            dma((3,)),
        ],
        compiler_params=pltpu.CompilerParams(vmem_limit_bytes=60 * 1024 * 1024),
        cost_estimate=pl.CostEstimate(flops=70_000_000, bytes_accessed=4_000_000, transcendentals=0),
    )(owner, final, left_new, right_new)
    return direction.reshape(row_width, col_width, blocks).transpose(2, 0, 1), left_new, right_new


def solution(mesh):
    placed = (
        P(None, "fsdp", "rep"),
        P(),
        P(("rep", "fsdp"), None),
        P(("rep", "fsdp"), None),
        P(("rep", "fsdp"), None),
        P(("rep", "fsdp"), None),
    )
    return jax.shard_map(
        per_device,
        mesh=mesh,
        in_specs=placed,
        out_specs=(P(None, "fsdp", "rep"), P(("rep", "fsdp"), None), P(("rep", "fsdp"), None)),
        check_vma=False,
    )
```

```python
import functools

import jax
import jax.numpy as jnp
from jax import lax
from jax.experimental import pallas as pl
from jax.experimental.pallas import tpu as pltpu
from jax.sharding import PartitionSpec as P

MESH = pl.DeviceIdType.MESH
F32 = jnp.float32
BF16 = jnp.bfloat16
B = 1024
GROUP = 4
BETA = 0.9
EPS = 1e-06
NZ = 16
NF = 32
NQ = NF // GROUP
QUARTER = B // GROUP
LANES = 128
NT = (((1,), (1,)), ((), ()))
TN = (((0,), (0,)), ((), ()))
def halves(even, odd):
    lane = lax.broadcasted_iota(jnp.int32, even.shape, even.ndim - 1)
    low = lane < LANES // 2
    axis = even.ndim - 1
    top = jnp.where(low, even, pltpu.roll(odd, LANES // 2, axis))
    bottom = jnp.where(low, pltpu.roll(even, LANES // 2, axis), odd)
    return top, bottom


def kernel(
    owner_ref, grad_in, lf_in, rf_in, lr_in, rr_in,
    final, ln_out, rn_out,
    grad, wide, send_fwd, mid_fwd, raw, block, lroot, rroot, lfac, rfac,
    tpart, acc, gains, sums, send_back, mid_back, lnew, rnew, stop_fwd, stop_back,
    in_sem, out_sem, zf_s, zf_r, xf_s, xf_r, sib_s, sib_r, r_s, r_r,
    ex_s, ex_r, gain_s, gain_r, zb_s, zb_r, xb_s, xb_r, stop_r,
):
    z = lax.axis_index("rep")
    f = lax.axis_index("fsdp")
    core = f % 2
    xy = f // 2
    m = f % GROUP
    own_q = f // GROUP
    x = f // 8
    zq = z // 4
    sibling = f + 1 - 2 * core
    across = f + 2 - 4 * (m // 2)
    m_across = m + 2 - 4 * (m // 2)
    near = 1 + 2 * (1 - (z % 4) // 2)
    quads = [zq, (zq + near) % 4, (zq + 4 - near) % 4, (zq + 2) % 4]

    def local(src, dst, sem):
        return pltpu.make_async_copy(src, dst, sem)

    def remote(src, dst, send, recv, zd, fd):
        return pltpu.make_async_remote_copy(
            src_ref=src, dst_ref=dst, send_sem=send, recv_sem=recv,
            device_id=(zd, fd), device_id_type=MESH,
        )

    def await_bytes(ref, sem):
        pltpu.make_async_copy(ref, ref, sem).wait()

    loads = [
        local(grad_in, grad, in_sem.at[0]),
        local(lr_in, lroot, in_sem.at[1]),
        local(rr_in, rroot.at[m], in_sem.at[2]),
        local(lf_in, lfac, in_sem.at[3]),
        local(rf_in, rfac, in_sem.at[4]),
    ]
    for load in loads:
        load.start()
    barrier = pltpu.get_barrier_semaphore()

    def greet_plane(i, carry):
        pl.semaphore_signal(barrier, inc=1, device_id=(z, (f + i) % NF), device_id_type=MESH)
        return carry

    def greet_ring(i, carry):
        pl.semaphore_signal(barrier, inc=1, device_id=((z + i) % NZ, f), device_id_type=MESH)
        return carry

    lax.fori_loop(1, NZ, greet_ring, 0)
    lax.fori_loop(1, NF, greet_plane, 0)

    owner = owner_ref[...]
    slot_row = lax.broadcasted_iota(jnp.int32, (LANES, LANES), 0)
    pick = (jnp.broadcast_to(owner, (LANES, LANES)) == slot_row).astype(BF16)
    loads[0].wait()
    for t in range(16):
        piece = jnp.concatenate((grad[t * 64 : t * 64 + 64, :], grad[(16 + t) * 64 : (16 + t) * 64 + 64, :]), axis=0)
        wide[pl.ds(t, LANES, stride=16), :] = lax.dot_general(pick, piece, NT, preferred_element_type=F32)
    for zd in range(NZ):
        send_fwd[zd] = wide[zd * 128 : zd * 128 + 128, :].reshape(NQ, 16, LANES).astype(BF16)

    pl.semaphore_wait(barrier, NZ - 1 + NF - 1)

    way = 1 - 2 * core

    def send_z(send, mid, send_sem, recv_sem, step):
        zd = (z + step * way + NZ) % NZ
        remote(send.at[zd], mid.at[z], send_sem, recv_sem.at[z], zd, f).start()

    def send_stop(send, stop, send_sem, recv_sem):
        zd = (z + way + NZ) % NZ
        remote(send.at[(z + NZ // 2) % NZ], stop, send_sem, recv_sem, zd, f).start()

    def pass_stop(mid, stop, send_sem, stop_sem, recv_sem):
        await_bytes(stop, stop_sem)
        origin = (z - way + NZ) % NZ
        zd = (z + 7 * way + NZ) % NZ
        remote(stop, mid.at[origin], send_sem, recv_sem.at[origin], zd, f).start()

    def send_root(member, index, fd, parts):
        for part in parts:
            rows = rroot.at[member, pl.ds(part * 64, 64)]
            remote(rows, rows, r_s.at[index], r_r.at[index], z, fd).start()

    loads[2].wait()
    send_stop(send_fwd, stop_fwd, zf_s, stop_r.at[0])
    for step in range(1, 6):
        for sign in (1, -1):
            send_z(send_fwd, mid_fwd, zf_s, zf_r, sign * step)
        if step < 5:
            send_root(m, 0, across, (step - 1,))
    local(send_fwd.at[z], mid_fwd.at[z], zf_r.at[z]).start()
    send_root(m, 1, sibling, range(4))
    pass_stop(mid_fwd, stop_fwd, zf_s, stop_r.at[0], zf_r)

    def forward_xy(qd):
        for t in range(4):
            await_bytes(mid_fwd.at[qd * 4 + t], zf_r.at[qd * 4 + t])

        for i in range(NF // 2):
            chip = (xy + i) % (NF // 2)
            q = chip // 2
            src = mid_fwd.at[pl.ds(qd * 4, 4), q]
            dst = raw.at[xy, core, pl.ds(qd * 4, 4)]
            if i == 0:
                local(src, dst, xf_r.at[qd, x]).start()
            else:
                remote(src, dst, xf_s.at[qd], xf_r.at[qd, x], z, chip * 2 + core).start()

    def share(qd):
        for i in range(4):
            column = (x + i) % 4
            mine = raw.at[pl.ds(column * 4, 4), core, pl.ds(qd * 4, 4)]
            await_bytes(mine, xf_r.at[qd, column])
            remote(mine, mine, sib_s.at[qd], sib_r.at[qd], z, sibling).start()

    def gather_chunk(qd):
        await_bytes(raw.at[:, 1 - core, pl.ds(qd * 4, 4)], sib_r.at[qd])

        def unpack(i, carry):
            for pair in range(2):
                first = qd * 4 + 2 * pair
                even = raw[pl.ds(i * 2, 2), :, first].reshape(64, LANES)
                odd = raw[pl.ds(i * 2, 2), :, first + 1].reshape(64, LANES)
                top, bottom = halves(even, odd)
                rows = jnp.concatenate((top.reshape(4, 16, LANES), bottom.reshape(4, 16, LANES)), axis=1)
                at = pl.multiple_of(i * 128, 128)
                block[qd, pl.ds(at, 128), pair * LANES : (pair + 1) * LANES] = rows.reshape(128, LANES)
            return carry

        lax.fori_loop(0, NF // 4, unpack, 0)

    def left_product(qd):
        tpart[qd] = jnp.dot(lroot[...], block[qd], preferred_element_type=F32).astype(BF16)

    def right_part(qd, j):
        return lax.dot_general(
            tpart[qd], rroot[j, :, pl.ds(pl.multiple_of(qd * QUARTER, QUARTER), QUARTER)], NT,
            preferred_element_type=F32,
        )

    def right_product(qd, first=False):
        for j in range(GROUP):
            if first:
                acc[j] = right_part(qd, j)
            else:
                acc[j] += right_part(qd, j)

    def grad_squares(qd, total):
        rows = block[qd, pl.ds(pl.multiple_of(m * QUARTER, QUARTER), QUARTER), :].astype(F32)
        return total + jnp.sum((rows * rows).reshape(QUARTER // 8, 8, 2, LANES), axis=(0, 2))

    total = jnp.zeros((8, LANES), F32)
    forward_xy(quads[0])
    for step in (6, 7):
        for sign in (1, -1):
            send_z(send_fwd, mid_fwd, zf_s, zf_r, sign * step)
    forward_xy(quads[1])
    loads[1].wait()
    share(quads[0])
    forward_xy(quads[2])
    share(quads[1])
    gather_chunk(quads[0])
    left_product(quads[0])
    total = grad_squares(quads[0], total)
    await_bytes(rroot.at[m_across], r_r.at[0])
    send_root(m_across, 2, sibling, range(4))
    forward_xy(quads[3])
    share(quads[2])
    gather_chunk(quads[1])
    left_product(quads[1])
    total = grad_squares(quads[1], total)
    await_bytes(rroot.at[0], r_r.at[1])
    await_bytes(rroot.at[0], r_r.at[2])
    right_product(quads[0], first=True)
    right_product(quads[1])
    share(quads[3])
    gather_chunk(quads[2])
    left_product(quads[2])
    total = grad_squares(quads[2], total)
    right_product(quads[2])
    gather_chunk(quads[3])
    left_product(quads[3])

    prec_total = jnp.zeros((8, LANES), F32)
    for c in range(4):
        value = (acc[c] + right_part(quads[3], c)).astype(BF16)
        for pair in range(2):
            rows = value[:, pair * LANES : (pair + 1) * LANES].reshape(NQ, 2, 16, LANES)
            even, odd = halves(rows[:, 0].reshape(LANES, LANES), rows[:, 1].reshape(LANES, LANES))
            send_back[c * 4 + 2 * pair] = even.reshape(NQ, 16, LANES)
            send_back[c * 4 + 2 * pair + 1] = odd.reshape(NQ, 16, LANES)
        wider = value.astype(F32)
        prec_total += jnp.sum((wider * wider).reshape(QUARTER // 8, 8, 2, LANES), axis=(0, 2))

    sums[m, 0] = grad_squares(quads[3], total)
    sums[m, 1] = prec_total
    for step in range(1, GROUP):
        fd = own_q * GROUP + (m + step) % GROUP
        remote(sums.at[m], sums.at[m], ex_s.at[step - 1], ex_r.at[m], z, fd).start()
    send_stop(send_back, stop_back, zb_s, stop_r.at[1])
    for step in (1, 2, 3):
        for sign in (1, -1):
            send_z(send_back, mid_back, zb_s, zb_r, sign * step)
    local(send_back.at[z], mid_back.at[z], zb_r.at[z]).start()
    for step in range(1, GROUP):
        await_bytes(sums.at[0], ex_r.at[(m + step) % GROUP])
    grad_sq = jnp.sum(sums[0, 0] + sums[1, 0] + sums[2, 0] + sums[3, 0], keepdims=True)
    prec_sq = jnp.sum(sums[0, 1] + sums[1, 1] + sums[2, 1] + sums[3, 1], keepdims=True)
    gains[z] = jnp.broadcast_to(jnp.sqrt((grad_sq + EPS) / (prec_sq + EPS)), (1, LANES))
    for step in range(1, NZ):
        zd = (z + step) % NZ
        remote(gains.at[z], gains.at[z], gain_s, gain_r.at[z], zd, f).start()
    for step in (4, 5, 6, 7):
        for sign in (1, -1):
            send_z(send_back, mid_back, zb_s, zb_r, sign * step)
    pass_stop(mid_back, stop_back, zb_s, stop_r.at[1], zb_r)

    def back_xy(qd):
        for t in range(4):
            zs = qd * 4 + t
            await_bytes(mid_back.at[zs], zb_r.at[zs])

            @pl.when(zs != z)
            def _():
                await_bytes(gains.at[zs], gain_r.at[zs])

            mid_back[zs] = (mid_back[zs].astype(F32) * gains[zs].reshape(1, 1, LANES)).astype(BF16)
        for i in range(NQ):
            d = (f % NQ + i) % NQ
            fd = m * NQ + d
            src = mid_back.at[pl.ds(qd * 4, 4), d]
            dst = final.at[own_q, pl.ds(qd * 4, 4)]
            if i > 0:
                remote(src, dst, xb_s.at[qd], xb_r.at[qd], z, fd).start()
                continue

            @pl.when(x != m)
            def _():
                remote(src, dst, xb_s.at[qd], xb_r.at[qd], z, fd).start()

            @pl.when(x == m)
            def _():
                local(src, dst, xb_r.at[qd]).start()

    def gram_left():
        rows = pl.ds(pl.multiple_of(m * QUARTER, QUARTER), QUARTER)
        for j in range(GROUP):
            gram = jnp.zeros((QUARTER, QUARTER), F32)
            for c in range(4):
                gram += lax.dot_general(
                    block[c, rows, :], block[c, j * QUARTER : (j + 1) * QUARTER, :], NT, preferred_element_type=F32
                )
            cols = slice(j * QUARTER, (j + 1) * QUARTER)
            lnew[:, cols] = (BETA * lfac[:, cols].astype(F32) + (1.0 - BETA) / B * gram).astype(BF16)

    def gram_right():
        for j in range(GROUP):
            gram = lax.dot_general(block[m], block[j], TN, preferred_element_type=F32)
            cols = slice(j * QUARTER, (j + 1) * QUARTER)
            rnew[:, cols] = (BETA * rfac[:, cols].astype(F32) + (1.0 - BETA) / B * gram).astype(BF16)

    loads[3].wait()
    gram_left()
    stores = [local(lnew, ln_out, out_sem.at[0]), local(rnew, rn_out, out_sem.at[1])]
    stores[0].start()
    back_xy(quads[0])
    loads[4].wait()
    gram_right()
    stores[1].start()
    back_xy(quads[1])
    back_xy(quads[2])
    back_xy(quads[3])

    for qd in quads:
        await_bytes(final.at[:, pl.ds(qd * 4, 4)], xb_r.at[qd])

    await_bytes(send_fwd, zf_s)
    await_bytes(send_back, zb_s)
    for c in range(4):
        await_bytes(raw.at[pl.ds(0, 15), 0, pl.ds(0, 4)], xf_s.at[c])
        await_bytes(raw.at[:, 0, pl.ds(0, 4)], sib_s.at[c])

        @pl.when(x == m)
        def _():
            await_bytes(final.at[pl.ds(0, NQ - 1), pl.ds(0, 4)], xb_s.at[c])

        @pl.when(x != m)
        def _():
            await_bytes(final.at[:, pl.ds(0, 4)], xb_s.at[c])

    await_bytes(gains.at[pl.ds(0, NZ - 1)], gain_s)
    for i in range(3):
        await_bytes(rroot.at[0], r_s.at[i])
        await_bytes(sums.at[0], ex_s.at[i])
    stores[0].wait()
    stores[1].wait()


def finish(owner_ref, final, lnew, rnew, dir_out, ln_out, rn_out, rows_in, wide, dirv, lvmem, rvmem, in_sem, out_sem):
    loads = [pltpu.make_async_copy(final.at[q], rows_in.at[q], in_sem.at[q]) for q in range(NQ)]
    stores = [
        pltpu.make_async_copy(lvmem, ln_out, out_sem.at[0]),
        pltpu.make_async_copy(rvmem, rn_out, out_sem.at[1]),
        pltpu.make_async_copy(dirv, dir_out, out_sem.at[2]),
    ]
    loads.append(pltpu.make_async_copy(lnew, lvmem, in_sem.at[NQ]))
    loads.append(pltpu.make_async_copy(rnew, rvmem, in_sem.at[NQ + 1]))
    for copy in loads:
        copy.start()
    row = lax.broadcasted_iota(jnp.int32, (LANES, LANES), 0)
    slot_of = (row % NZ) * NQ + row // NZ
    place = (jnp.broadcast_to(owner_ref[...], (LANES, LANES)) == slot_of).astype(BF16)
    for q in range(NQ):
        loads[q].wait()
        wide[q * 256 : q * 256 + 256, :] = rows_in[q].reshape(256, LANES).astype(F32)
    for i in range(2):
        loads[NQ + i].wait()
        stores[i].start()
    for t in range(16):
        rows = wide[pl.ds(t, LANES, stride=16), :].astype(BF16)
        blocks = lax.dot_general(rows, place, TN, preferred_element_type=F32).astype(BF16)
        dirv[t * 64 : t * 64 + 64, :] = blocks[:64]
        dirv[(16 + t) * 64 : (16 + t) * 64 + 64, :] = blocks[64:]
    stores[2].start()
    for copy in stores:
        copy.wait()


def per_device(gradient, owner_slot, left_factor, right_factor, left_root, right_root):
    blocks, row_width, col_width = gradient.shape
    columns = gradient.transpose(1, 2, 0).reshape(row_width * col_width, blocks)
    anywhere = pl.BlockSpec(memory_space=pl.ANY)
    factor = jax.ShapeDtypeStruct((QUARTER, B), BF16)
    dma = pltpu.SemaphoreType.DMA
    owner = owner_slot.reshape(1, blocks)
    final, left_new, right_new = pl.pallas_call(
        kernel,
        out_shape=(jax.ShapeDtypeStruct((NQ, NZ, 16, LANES), BF16), factor, factor),
        in_specs=[pl.BlockSpec(memory_space=pltpu.VMEM)] + [anywhere] * 5,
        out_specs=(anywhere, anywhere, anywhere),
        scratch_shapes=[
            pltpu.VMEM((2048, LANES), BF16),
            pltpu.VMEM((2048, LANES), F32),
            pltpu.VMEM((NZ, NQ, 16, LANES), BF16),
            pltpu.VMEM((NZ, NQ, 16, LANES), BF16),
            pltpu.VMEM((NF // 2, 2, NZ, 16, LANES), BF16),
            pltpu.VMEM((4, B, QUARTER), BF16),
            pltpu.VMEM((QUARTER, B), BF16),
            pltpu.VMEM((GROUP, QUARTER, B), BF16),
            pltpu.VMEM((QUARTER, B), BF16),
            pltpu.VMEM((QUARTER, B), BF16),
            pltpu.VMEM((4, QUARTER, QUARTER), BF16),
            pltpu.VMEM((GROUP, QUARTER, QUARTER), F32),
            pltpu.VMEM((NZ, 1, LANES), F32),
            pltpu.VMEM((GROUP, 2, 8, LANES), F32),
            pltpu.VMEM((NZ, NQ, 16, LANES), BF16),
            pltpu.VMEM((NZ, NQ, 16, LANES), BF16),
            pltpu.VMEM((QUARTER, B), BF16),
            pltpu.VMEM((QUARTER, B), BF16),
            pltpu.VMEM((NQ, 16, LANES), BF16),
            pltpu.VMEM((NQ, 16, LANES), BF16),
            dma((5,)), dma((2,)),
            dma, dma((NZ,)),
            dma((4,)), dma((4, 4)),
            dma((4,)), dma((4,)),
            dma((3,)), dma((3,)),
            dma((3,)), dma((GROUP,)),
            dma, dma((NZ,)),
            dma, dma((NZ,)),
            dma((4,)), dma((4,)),
            dma((2,)),
        ],
        compiler_params=pltpu.CompilerParams(
            collective_id=0, has_side_effects=True, vmem_limit_bytes=60 * 1024 * 1024
        ),
        cost_estimate=pl.CostEstimate(flops=2_200_000_000, bytes_accessed=8_000_000, transcendentals=0),
    )(owner, columns, left_factor, right_factor, left_root, right_root)
    direction, left_new, right_new = pl.pallas_call(
        finish,
        out_shape=(jax.ShapeDtypeStruct(columns.shape, BF16), factor, factor),
        in_specs=[pl.BlockSpec(memory_space=pltpu.VMEM)] + [anywhere] * 3,
        out_specs=(anywhere, anywhere, anywhere),
        scratch_shapes=[
            pltpu.VMEM((NQ, NZ, 16, LANES), BF16),
            pltpu.VMEM((2048, LANES), F32),
            pltpu.VMEM((2048, LANES), BF16),
            pltpu.VMEM((QUARTER, B), BF16),
            pltpu.VMEM((QUARTER, B), BF16),
            dma((NQ + 2,)),
            dma((3,)),
        ],
        compiler_params=pltpu.CompilerParams(vmem_limit_bytes=60 * 1024 * 1024),
        cost_estimate=pl.CostEstimate(flops=70_000_000, bytes_accessed=4_000_000, transcendentals=0),
    )(owner, final, left_new, right_new)
    return direction.reshape(row_width, col_width, blocks).transpose(2, 0, 1), left_new, right_new


def solution(mesh):
    placed = (
        P(None, "fsdp", "rep"),
        P(),
        P(("rep", "fsdp"), None),
        P(("rep", "fsdp"), None),
        P(("rep", "fsdp"), None),
        P(("rep", "fsdp"), None),
    )
    return jax.shard_map(
        per_device,
        mesh=mesh,
        in_specs=placed,
        out_specs=(P(None, "fsdp", "rep"), P(("rep", "fsdp"), None), P(("rep", "fsdp"), None)),
        check_vma=False,
    )
```

```python
import functools

import jax
import jax.numpy as jnp
from jax import lax
from jax.experimental import pallas as pl
from jax.experimental.pallas import tpu as pltpu
from jax.sharding import PartitionSpec as P

MESH = pl.DeviceIdType.MESH
F32 = jnp.float32
BF16 = jnp.bfloat16
B = 1024
GROUP = 4
BETA = 0.9
EPS = 1e-06
NZ = 16
NF = 32
NQ = NF // GROUP
QUARTER = B // GROUP
LANES = 128
NT = (((1,), (1,)), ((), ()))
TN = (((0,), (0,)), ((), ()))
def halves(even, odd):
    lane = lax.broadcasted_iota(jnp.int32, even.shape, even.ndim - 1)
    low = lane < LANES // 2
    axis = even.ndim - 1
    top = jnp.where(low, even, pltpu.roll(odd, LANES // 2, axis))
    bottom = jnp.where(low, pltpu.roll(even, LANES // 2, axis), odd)
    return top, bottom


def kernel(
    owner_ref, grad_in, lf_in, rf_in, lr_in, rr_in,
    final, ln_out, rn_out,
    grad, wide, send_fwd, mid_fwd, raw, block, lroot, rroot, lfac, rfac,
    tpart, acc, gains, sums, send_back, mid_back, lnew, rnew, stop_fwd, stop_back,
    in_sem, out_sem, zf_s, zf_r, xf_s, xf_r, sib_s, sib_r, r_s, r_r,
    ex_s, ex_r, gain_s, gain_r, zb_s, zb_r, xb_s, xb_r, stop_r,
):
    z = lax.axis_index("rep")
    f = lax.axis_index("fsdp")
    core = f % 2
    xy = f // 2
    m = f % GROUP
    own_q = f // GROUP
    x = f // 8
    zq = z // 4
    sibling = f + 1 - 2 * core
    across = f + 2 - 4 * (m // 2)
    m_across = m + 2 - 4 * (m // 2)
    near = 1 + 2 * (1 - (z % 4) // 2)
    quads = [zq, (zq + near) % 4, (zq + 4 - near) % 4, (zq + 2) % 4]

    def local(src, dst, sem):
        return pltpu.make_async_copy(src, dst, sem)

    def remote(src, dst, send, recv, zd, fd):
        return pltpu.make_async_remote_copy(
            src_ref=src, dst_ref=dst, send_sem=send, recv_sem=recv,
            device_id=(zd, fd), device_id_type=MESH,
        )

    def await_bytes(ref, sem):
        pltpu.make_async_copy(ref, ref, sem).wait()

    loads = [
        local(grad_in, grad, in_sem.at[0]),
        local(lr_in, lroot, in_sem.at[1]),
        local(rr_in, rroot.at[m], in_sem.at[2]),
        local(lf_in, lfac, in_sem.at[3]),
        local(rf_in, rfac, in_sem.at[4]),
    ]
    for load in loads:
        load.start()
    barrier = pltpu.get_barrier_semaphore()

    def greet_plane(i, carry):
        pl.semaphore_signal(barrier, inc=1, device_id=(z, (f + i) % NF), device_id_type=MESH)
        return carry

    def greet_ring(i, carry):
        pl.semaphore_signal(barrier, inc=1, device_id=((z + i) % NZ, f), device_id_type=MESH)
        return carry

    lax.fori_loop(1, NZ, greet_ring, 0)
    lax.fori_loop(1, NF, greet_plane, 0)

    owner = owner_ref[...]
    slot_row = lax.broadcasted_iota(jnp.int32, (LANES, LANES), 0)
    pick = (jnp.broadcast_to(owner, (LANES, LANES)) == slot_row).astype(BF16)
    loads[0].wait()
    for t in range(16):
        piece = jnp.concatenate((grad[t * 64 : t * 64 + 64, :], grad[(16 + t) * 64 : (16 + t) * 64 + 64, :]), axis=0)
        wide[pl.ds(t, LANES, stride=16), :] = lax.dot_general(pick, piece, NT, preferred_element_type=F32)
    for zd in range(NZ):
        send_fwd[zd] = wide[zd * 128 : zd * 128 + 128, :].reshape(NQ, 16, LANES).astype(BF16)

    pl.semaphore_wait(barrier, NZ - 1 + NF - 1)

    way = 1 - 2 * core

    def send_z(send, mid, send_sem, recv_sem, step):
        if step > 2:
            await_bytes(send.at[pl.ds(0, 2)], send_sem.at[step - 2])
        for sign in (1, -1):
            zd = (z + sign * step * way + NZ) % NZ
            remote(send.at[zd], mid.at[z], send_sem.at[step], recv_sem.at[z], zd, f).start()

    def send_stop(send, stop, send_sem, recv_sem):
        zd = (z + way + NZ) % NZ
        remote(send.at[(z + NZ // 2) % NZ], stop, send_sem.at[0], recv_sem, zd, f).start()

    def pass_stop(mid, stop, send_sem, stop_sem, recv_sem):
        await_bytes(stop, stop_sem)
        origin = (z - way + NZ) % NZ
        zd = (z + 7 * way + NZ) % NZ
        remote(stop, mid.at[origin], send_sem.at[0], recv_sem.at[origin], zd, f).start()

    def send_root(member, index, fd, parts):
        for part in parts:
            rows = rroot.at[member, pl.ds(part * 64, 64)]
            remote(rows, rows, r_s.at[index], r_r.at[index], z, fd).start()

    loads[2].wait()
    def hop_fwd(step):
        send_z(send_fwd, mid_fwd, zf_s, zf_r, step)

    def hop_back(step):
        send_z(send_back, mid_back, zb_s, zb_r, step)

    send_stop(send_fwd, stop_fwd, zf_s, stop_r.at[0])
    hop_fwd(1)
    send_root(m, 0, across, (0,))
    hop_fwd(2)
    send_root(m, 0, across, (1,))
    local(send_fwd.at[z], mid_fwd.at[z], zf_r.at[z]).start()
    hop_fwd(3)
    send_root(m, 0, across, (2,))
    pass_stop(mid_fwd, stop_fwd, zf_s, stop_r.at[0], zf_r)
    hop_fwd(4)
    send_root(m, 0, across, (3,))
    send_root(m, 1, sibling, range(4))
    hop_fwd(5)

    def forward_xy(qd):
        for t in range(4):
            await_bytes(mid_fwd.at[qd * 4 + t], zf_r.at[qd * 4 + t])

        for i in range(NF // 2):
            chip = (xy + i) % (NF // 2)
            q = chip // 2
            src = mid_fwd.at[pl.ds(qd * 4, 4), q]
            dst = raw.at[xy, core, pl.ds(qd * 4, 4)]
            if i == 0:
                local(src, dst, xf_r.at[qd, x]).start()
            else:
                remote(src, dst, xf_s.at[qd], xf_r.at[qd, x], z, chip * 2 + core).start()

    def share(qd):
        for i in range(4):
            column = (x + i) % 4
            mine = raw.at[pl.ds(column * 4, 4), core, pl.ds(qd * 4, 4)]
            await_bytes(mine, xf_r.at[qd, column])
            remote(mine, mine, sib_s.at[qd], sib_r.at[qd], z, sibling).start()

    def gather_chunk(qd):
        await_bytes(raw.at[:, 1 - core, pl.ds(qd * 4, 4)], sib_r.at[qd])

        def unpack(i, carry):
            for pair in range(2):
                first = qd * 4 + 2 * pair
                even = raw[pl.ds(i * 2, 2), :, first].reshape(64, LANES)
                odd = raw[pl.ds(i * 2, 2), :, first + 1].reshape(64, LANES)
                top, bottom = halves(even, odd)
                rows = jnp.concatenate((top.reshape(4, 16, LANES), bottom.reshape(4, 16, LANES)), axis=1)
                at = pl.multiple_of(i * 128, 128)
                block[qd, pl.ds(at, 128), pair * LANES : (pair + 1) * LANES] = rows.reshape(128, LANES)
            return carry

        lax.fori_loop(0, NF // 4, unpack, 0)

    def left_product(qd):
        tpart[qd] = jnp.dot(lroot[...], block[qd], preferred_element_type=F32).astype(BF16)

    def right_part(qd, j):
        return lax.dot_general(
            tpart[qd], rroot[j, :, pl.ds(pl.multiple_of(qd * QUARTER, QUARTER), QUARTER)], NT,
            preferred_element_type=F32,
        )

    def right_product(qd, first=False):
        for j in range(GROUP):
            if first:
                acc[j] = right_part(qd, j)
            else:
                acc[j] += right_part(qd, j)

    def grad_squares(qd, total):
        rows = block[qd, pl.ds(pl.multiple_of(m * QUARTER, QUARTER), QUARTER), :].astype(F32)
        return total + jnp.sum((rows * rows).reshape(QUARTER // 8, 8, 2, LANES), axis=(0, 2))

    total = jnp.zeros((8, LANES), F32)
    forward_xy(quads[0])
    hop_fwd(6)
    loads[1].wait()
    hop_fwd(7)
    forward_xy(quads[1])
    share(quads[0])
    await_bytes(rroot.at[m_across], r_r.at[0])
    send_root(m_across, 2, sibling, range(4))
    forward_xy(quads[2])
    share(quads[1])
    forward_xy(quads[3])
    gather_chunk(quads[0])
    left_product(quads[0])
    total = grad_squares(quads[0], total)
    share(quads[2])
    gather_chunk(quads[1])
    left_product(quads[1])
    total = grad_squares(quads[1], total)
    await_bytes(rroot.at[0], r_r.at[1])
    await_bytes(rroot.at[0], r_r.at[2])
    right_product(quads[0], first=True)
    right_product(quads[1])
    share(quads[3])
    gather_chunk(quads[2])
    left_product(quads[2])
    total = grad_squares(quads[2], total)
    right_product(quads[2])
    gather_chunk(quads[3])
    left_product(quads[3])

    prec_total = jnp.zeros((8, LANES), F32)
    for c in range(4):
        value = (acc[c] + right_part(quads[3], c)).astype(BF16)
        for pair in range(2):
            rows = value[:, pair * LANES : (pair + 1) * LANES].reshape(NQ, 2, 16, LANES)
            even, odd = halves(rows[:, 0].reshape(LANES, LANES), rows[:, 1].reshape(LANES, LANES))
            send_back[c * 4 + 2 * pair] = even.reshape(NQ, 16, LANES)
            send_back[c * 4 + 2 * pair + 1] = odd.reshape(NQ, 16, LANES)
        wider = value.astype(F32)
        prec_total += jnp.sum((wider * wider).reshape(QUARTER // 8, 8, 2, LANES), axis=(0, 2))

    sums[m, 0] = grad_squares(quads[3], total)
    sums[m, 1] = prec_total
    for step in range(1, GROUP):
        fd = own_q * GROUP + (m + step) % GROUP
        remote(sums.at[m], sums.at[m], ex_s.at[step - 1], ex_r.at[m], z, fd).start()
    send_stop(send_back, stop_back, zb_s, stop_r.at[1])
    hop_back(1)
    hop_back(2)
    local(send_back.at[z], mid_back.at[z], zb_r.at[z]).start()
    for step in range(1, GROUP):
        await_bytes(sums.at[0], ex_r.at[(m + step) % GROUP])
    grad_sq = jnp.sum(sums[0, 0] + sums[1, 0] + sums[2, 0] + sums[3, 0], keepdims=True)
    prec_sq = jnp.sum(sums[0, 1] + sums[1, 1] + sums[2, 1] + sums[3, 1], keepdims=True)
    gains[z] = jnp.broadcast_to(jnp.sqrt((grad_sq + EPS) / (prec_sq + EPS)), (1, LANES))
    for step in range(1, NZ):
        zd = (z + step) % NZ
        remote(gains.at[z], gains.at[z], gain_s, gain_r.at[z], zd, f).start()
    hop_back(3)
    hop_back(4)
    pass_stop(mid_back, stop_back, zb_s, stop_r.at[1], zb_r)

    def back_xy(qd):
        for t in range(4):
            zs = qd * 4 + t
            await_bytes(mid_back.at[zs], zb_r.at[zs])

            @pl.when(zs != z)
            def _():
                await_bytes(gains.at[zs], gain_r.at[zs])

            mid_back[zs] = (mid_back[zs].astype(F32) * gains[zs].reshape(1, 1, LANES)).astype(BF16)
        for i in range(NQ):
            d = (f % NQ + i) % NQ
            fd = m * NQ + d
            src = mid_back.at[pl.ds(qd * 4, 4), d]
            dst = final.at[own_q, pl.ds(qd * 4, 4)]
            if i > 0:
                remote(src, dst, xb_s.at[qd], xb_r.at[qd], z, fd).start()
                continue

            @pl.when(x != m)
            def _():
                remote(src, dst, xb_s.at[qd], xb_r.at[qd], z, fd).start()

            @pl.when(x == m)
            def _():
                local(src, dst, xb_r.at[qd]).start()

    def gram_left():
        rows = pl.ds(pl.multiple_of(m * QUARTER, QUARTER), QUARTER)
        for j in range(GROUP):
            gram = jnp.zeros((QUARTER, QUARTER), F32)
            for c in range(4):
                gram += lax.dot_general(
                    block[c, rows, :], block[c, j * QUARTER : (j + 1) * QUARTER, :], NT, preferred_element_type=F32
                )
            cols = slice(j * QUARTER, (j + 1) * QUARTER)
            lnew[:, cols] = (BETA * lfac[:, cols].astype(F32) + (1.0 - BETA) / B * gram).astype(BF16)

    def gram_right():
        for j in range(GROUP):
            gram = lax.dot_general(block[m], block[j], TN, preferred_element_type=F32)
            cols = slice(j * QUARTER, (j + 1) * QUARTER)
            rnew[:, cols] = (BETA * rfac[:, cols].astype(F32) + (1.0 - BETA) / B * gram).astype(BF16)

    loads[3].wait()
    gram_left()
    stores = [local(lnew, ln_out, out_sem.at[0]), local(rnew, rn_out, out_sem.at[1])]
    stores[0].start()
    hop_back(5)
    back_xy(quads[0])
    hop_back(6)
    loads[4].wait()
    gram_right()
    stores[1].start()
    hop_back(7)
    back_xy(quads[1])
    back_xy(quads[2])
    back_xy(quads[3])

    for qd in quads:
        await_bytes(final.at[:, pl.ds(qd * 4, 4)], xb_r.at[qd])

    for sem in (zf_s, zb_s):
        for step in (0, 6, 7):
            await_bytes(send_fwd.at[pl.ds(0, 2)], sem.at[step])
    for c in range(4):
        await_bytes(raw.at[pl.ds(0, 15), 0, pl.ds(0, 4)], xf_s.at[c])
        await_bytes(raw.at[:, 0, pl.ds(0, 4)], sib_s.at[c])

        @pl.when(x == m)
        def _():
            await_bytes(final.at[pl.ds(0, NQ - 1), pl.ds(0, 4)], xb_s.at[c])

        @pl.when(x != m)
        def _():
            await_bytes(final.at[:, pl.ds(0, 4)], xb_s.at[c])

    await_bytes(gains.at[pl.ds(0, NZ - 1)], gain_s)
    for i in range(3):
        await_bytes(rroot.at[0], r_s.at[i])
        await_bytes(sums.at[0], ex_s.at[i])
    stores[0].wait()
    stores[1].wait()


def finish(owner_ref, final, lnew, rnew, dir_out, ln_out, rn_out, rows_in, wide, dirv, lvmem, rvmem, in_sem, out_sem):
    loads = [pltpu.make_async_copy(final.at[q], rows_in.at[q], in_sem.at[q]) for q in range(NQ)]
    stores = [
        pltpu.make_async_copy(lvmem, ln_out, out_sem.at[0]),
        pltpu.make_async_copy(rvmem, rn_out, out_sem.at[1]),
        pltpu.make_async_copy(dirv, dir_out, out_sem.at[2]),
    ]
    loads.append(pltpu.make_async_copy(lnew, lvmem, in_sem.at[NQ]))
    loads.append(pltpu.make_async_copy(rnew, rvmem, in_sem.at[NQ + 1]))
    for copy in loads:
        copy.start()
    row = lax.broadcasted_iota(jnp.int32, (LANES, LANES), 0)
    slot_of = (row % NZ) * NQ + row // NZ
    place = (jnp.broadcast_to(owner_ref[...], (LANES, LANES)) == slot_of).astype(BF16)
    for q in range(NQ):
        loads[q].wait()
        wide[q * 256 : q * 256 + 256, :] = rows_in[q].reshape(256, LANES).astype(F32)
    for i in range(2):
        loads[NQ + i].wait()
        stores[i].start()
    for t in range(16):
        rows = wide[pl.ds(t, LANES, stride=16), :].astype(BF16)
        blocks = lax.dot_general(rows, place, TN, preferred_element_type=F32).astype(BF16)
        dirv[t * 64 : t * 64 + 64, :] = blocks[:64]
        dirv[(16 + t) * 64 : (16 + t) * 64 + 64, :] = blocks[64:]
    stores[2].start()
    for copy in stores:
        copy.wait()


def per_device(gradient, owner_slot, left_factor, right_factor, left_root, right_root):
    blocks, row_width, col_width = gradient.shape
    columns = gradient.transpose(1, 2, 0).reshape(row_width * col_width, blocks)
    anywhere = pl.BlockSpec(memory_space=pl.ANY)
    factor = jax.ShapeDtypeStruct((QUARTER, B), BF16)
    dma = pltpu.SemaphoreType.DMA
    owner = owner_slot.reshape(1, blocks)
    final, left_new, right_new = pl.pallas_call(
        kernel,
        out_shape=(jax.ShapeDtypeStruct((NQ, NZ, 16, LANES), BF16), factor, factor),
        in_specs=[pl.BlockSpec(memory_space=pltpu.VMEM)] + [anywhere] * 5,
        out_specs=(anywhere, anywhere, anywhere),
        scratch_shapes=[
            pltpu.VMEM((2048, LANES), BF16),
            pltpu.VMEM((2048, LANES), F32),
            pltpu.VMEM((NZ, NQ, 16, LANES), BF16),
            pltpu.VMEM((NZ, NQ, 16, LANES), BF16),
            pltpu.VMEM((NF // 2, 2, NZ, 16, LANES), BF16),
            pltpu.VMEM((4, B, QUARTER), BF16),
            pltpu.VMEM((QUARTER, B), BF16),
            pltpu.VMEM((GROUP, QUARTER, B), BF16),
            pltpu.VMEM((QUARTER, B), BF16),
            pltpu.VMEM((QUARTER, B), BF16),
            pltpu.VMEM((4, QUARTER, QUARTER), BF16),
            pltpu.VMEM((GROUP, QUARTER, QUARTER), F32),
            pltpu.VMEM((NZ, 1, LANES), F32),
            pltpu.VMEM((GROUP, 2, 8, LANES), F32),
            pltpu.VMEM((NZ, NQ, 16, LANES), BF16),
            pltpu.VMEM((NZ, NQ, 16, LANES), BF16),
            pltpu.VMEM((QUARTER, B), BF16),
            pltpu.VMEM((QUARTER, B), BF16),
            pltpu.VMEM((NQ, 16, LANES), BF16),
            pltpu.VMEM((NQ, 16, LANES), BF16),
            dma((5,)), dma((2,)),
            dma((8,)), dma((NZ,)),
            dma((4,)), dma((4, 4)),
            dma((4,)), dma((4,)),
            dma((3,)), dma((3,)),
            dma((3,)), dma((GROUP,)),
            dma, dma((NZ,)),
            dma((8,)), dma((NZ,)),
            dma((4,)), dma((4,)),
            dma((2,)),
        ],
        compiler_params=pltpu.CompilerParams(
            collective_id=0, has_side_effects=True, vmem_limit_bytes=60 * 1024 * 1024
        ),
        cost_estimate=pl.CostEstimate(flops=2_200_000_000, bytes_accessed=8_000_000, transcendentals=0),
    )(owner, columns, left_factor, right_factor, left_root, right_root)
    direction, left_new, right_new = pl.pallas_call(
        finish,
        out_shape=(jax.ShapeDtypeStruct(columns.shape, BF16), factor, factor),
        in_specs=[pl.BlockSpec(memory_space=pltpu.VMEM)] + [anywhere] * 3,
        out_specs=(anywhere, anywhere, anywhere),
        scratch_shapes=[
            pltpu.VMEM((NQ, NZ, 16, LANES), BF16),
            pltpu.VMEM((2048, LANES), F32),
            pltpu.VMEM((2048, LANES), BF16),
            pltpu.VMEM((QUARTER, B), BF16),
            pltpu.VMEM((QUARTER, B), BF16),
            dma((NQ + 2,)),
            dma((3,)),
        ],
        compiler_params=pltpu.CompilerParams(vmem_limit_bytes=60 * 1024 * 1024),
        cost_estimate=pl.CostEstimate(flops=70_000_000, bytes_accessed=4_000_000, transcendentals=0),
    )(owner, final, left_new, right_new)
    return direction.reshape(row_width, col_width, blocks).transpose(2, 0, 1), left_new, right_new


def solution(mesh):
    placed = (
        P(None, "fsdp", "rep"),
        P(),
        P(("rep", "fsdp"), None),
        P(("rep", "fsdp"), None),
        P(("rep", "fsdp"), None),
        P(("rep", "fsdp"), None),
    )
    return jax.shard_map(
        per_device,
        mesh=mesh,
        in_specs=placed,
        out_specs=(P(None, "fsdp", "rep"), P(("rep", "fsdp"), None), P(("rep", "fsdp"), None)),
        check_vma=False,
    )
```

```python
import functools

import jax
import jax.numpy as jnp
from jax import lax
from jax.experimental import pallas as pl
from jax.experimental.pallas import tpu as pltpu
from jax.sharding import PartitionSpec as P

MESH = pl.DeviceIdType.MESH
F32 = jnp.float32
BF16 = jnp.bfloat16
B = 1024
GROUP = 4
BETA = 0.9
EPS = 1e-06
NZ = 16
NF = 32
NQ = NF // GROUP
QUARTER = B // GROUP
LANES = 128
NT = (((1,), (1,)), ((), ()))
TN = (((0,), (0,)), ((), ()))
def halves(even, odd):
    lane = lax.broadcasted_iota(jnp.int32, even.shape, even.ndim - 1)
    low = lane < LANES // 2
    axis = even.ndim - 1
    top = jnp.where(low, even, pltpu.roll(odd, LANES // 2, axis))
    bottom = jnp.where(low, pltpu.roll(even, LANES // 2, axis), odd)
    return top, bottom


def kernel(
    owner_ref, grad_in, lf_in, rf_in, lr_in, rr_in,
    final, ln_out, rn_out,
    grad, wide, send_fwd, mid_fwd, raw, block, lroot, rroot, lfac, rfac,
    tpart, acc, gains, sums, send_back, mid_back, lnew, rnew, stop_fwd, stop_back,
    in_sem, out_sem, zf_s, zf_r, xf_s, xf_r, sib_s, sib_r, r_s, r_r,
    ex_s, ex_r, gain_s, gain_r, zb_s, zb_r, xb_s, xb_r, stop_r,
):
    z = lax.axis_index("rep")
    f = lax.axis_index("fsdp")
    core = f % 2
    xy = f // 2
    m = f % GROUP
    own_q = f // GROUP
    x = f // 8
    zq = z // 4
    sibling = f + 1 - 2 * core
    across = f + 2 - 4 * (m // 2)
    m_across = m + 2 - 4 * (m // 2)
    near = 1 + 2 * (1 - (z % 4) // 2)
    quads = [zq, (zq + near) % 4, (zq + 4 - near) % 4, (zq + 2) % 4]

    def local(src, dst, sem):
        return pltpu.make_async_copy(src, dst, sem)

    def remote(src, dst, send, recv, zd, fd):
        return pltpu.make_async_remote_copy(
            src_ref=src, dst_ref=dst, send_sem=send, recv_sem=recv,
            device_id=(zd, fd), device_id_type=MESH,
        )

    def await_bytes(ref, sem):
        pltpu.make_async_copy(ref, ref, sem).wait()

    loads = [
        local(grad_in, grad, in_sem.at[0]),
        local(lr_in, lroot, in_sem.at[1]),
        local(rr_in, rroot.at[m], in_sem.at[2]),
        local(lf_in, lfac, in_sem.at[3]),
        local(rf_in, rfac, in_sem.at[4]),
    ]
    for load in loads:
        load.start()
    barrier = pltpu.get_barrier_semaphore()

    def greet_plane(i, carry):
        pl.semaphore_signal(barrier, inc=1, device_id=(z, (f + i) % NF), device_id_type=MESH)
        return carry

    def greet_ring(i, carry):
        pl.semaphore_signal(barrier, inc=1, device_id=((z + i) % NZ, f), device_id_type=MESH)
        return carry

    lax.fori_loop(1, NZ, greet_ring, 0)
    lax.fori_loop(1, NF, greet_plane, 0)

    owner = owner_ref[...]
    slot_row = lax.broadcasted_iota(jnp.int32, (LANES, LANES), 0)
    pick = (jnp.broadcast_to(owner, (LANES, LANES)) == slot_row).astype(BF16)
    loads[0].wait()
    for t in range(16):
        piece = jnp.concatenate((grad[t * 64 : t * 64 + 64, :], grad[(16 + t) * 64 : (16 + t) * 64 + 64, :]), axis=0)
        wide[pl.ds(t, LANES, stride=16), :] = lax.dot_general(pick, piece, NT, preferred_element_type=F32)
    for zd in range(NZ):
        send_fwd[zd] = wide[zd * 128 : zd * 128 + 128, :].reshape(NQ, 16, LANES).astype(BF16)

    pl.semaphore_wait(barrier, NZ - 1 + NF - 1)

    way = 1 - 2 * core

    def by_parity(plane):
        return plane % 2 * 8 + plane // 2

    def opposite(send, stop, send_sem, recv_sem):
        zd = (z + way + NZ) % NZ
        remote(send.at[(z + NZ // 2) % NZ], stop, send_sem, recv_sem, zd, f).start()

    def pass_stop(mid, slot, stop, send_sem, stop_sem, recv_sem):
        await_bytes(stop, stop_sem)
        zd = (z + 7 * way + NZ) % NZ
        remote(stop, mid.at[slot], send_sem, recv_sem.at[slot], zd, f).start()

    behind = (z - way + NZ) % NZ

    def send_root(member, index, fd, parts):
        for part in parts:
            rows = rroot.at[member, pl.ds(part * 64, 64)]
            remote(rows, rows, r_s.at[index], r_r.at[index], z, fd).start()

    loads[2].wait()
    odd_z = z % 2

    def both_fwd(step, sem):
        for sign in (1, -1):
            zd = (z + sign * step * way + NZ) % NZ
            remote(send_fwd.at[zd], mid_fwd.at[z], zf_s.at[sem], zf_r.at[z], zd, f).start()

    def group_fwd(phase, i):
        sem = phase * 4 + i
        if sem in (2, 3, 4, 6, 7):
            await_bytes(send_fwd.at[pl.ds(0, 2)], zf_s.at[sem - 2 if sem != 4 else 2])
        flip = odd_z if phase == 0 else 1 - odd_z
        if i < 3:
            both_fwd(2 * (i + 1) - flip, sem)
            return

        @pl.when(flip == 1)
        def _():
            both_fwd(7, sem)

        @pl.when(flip == 0)
        def _():
            opposite(send_fwd, stop_fwd, zf_s.at[sem], stop_r.at[0])

    group_fwd(0, 0)
    send_root(m, 0, across, (0,))
    group_fwd(0, 1)
    send_root(m, 0, across, (1,))
    local(send_fwd.at[z], mid_fwd.at[z], zf_r.at[z]).start()
    group_fwd(0, 2)
    send_root(m, 0, across, (2,))
    group_fwd(0, 3)
    send_root(m, 0, across, (3,))
    send_root(m, 1, sibling, range(4))

    @pl.when(odd_z == 1)
    def _():
        pass_stop(mid_fwd, behind, stop_fwd, zf_s.at[8], stop_r.at[0], zf_r)

    group_fwd(1, 0)
    group_fwd(1, 1)

    def forward_xy(qd):
        for t in range(4):
            await_bytes(mid_fwd.at[qd * 4 + t], zf_r.at[qd * 4 + t])

        for i in range(NF // 2):
            chip = (xy + i) % (NF // 2)
            q = chip // 2
            src = mid_fwd.at[pl.ds(qd * 4, 4), q]
            dst = raw.at[xy, core, pl.ds(qd * 4, 4)]
            if i == 0:
                local(src, dst, xf_r.at[qd, x]).start()
            else:
                remote(src, dst, xf_s.at[qd], xf_r.at[qd, x], z, chip * 2 + core).start()

    def share(qd):
        for i in range(4):
            column = (x + i) % 4
            mine = raw.at[pl.ds(column * 4, 4), core, pl.ds(qd * 4, 4)]
            await_bytes(mine, xf_r.at[qd, column])
            remote(mine, mine, sib_s.at[qd], sib_r.at[qd], z, sibling).start()

    def gather_chunk(qd):
        await_bytes(raw.at[:, 1 - core, pl.ds(qd * 4, 4)], sib_r.at[qd])

        def unpack(i, carry):
            for pair in range(2):
                first = qd * 4 + 2 * pair
                even = raw[pl.ds(i * 2, 2), :, first].reshape(64, LANES)
                odd = raw[pl.ds(i * 2, 2), :, first + 1].reshape(64, LANES)
                top, bottom = halves(even, odd)
                rows = jnp.concatenate((top.reshape(4, 16, LANES), bottom.reshape(4, 16, LANES)), axis=1)
                at = pl.multiple_of(i * 128, 128)
                block[qd, pl.ds(at, 128), pair * LANES : (pair + 1) * LANES] = rows.reshape(128, LANES)
            return carry

        lax.fori_loop(0, NF // 4, unpack, 0)

    def left_product(qd):
        tpart[qd] = jnp.dot(lroot[...], block[qd], preferred_element_type=F32).astype(BF16)

    def right_part(qd, j):
        return lax.dot_general(
            tpart[qd], rroot[j, :, pl.ds(pl.multiple_of(qd * QUARTER, QUARTER), QUARTER)], NT,
            preferred_element_type=F32,
        )

    def right_product(qd, first=False):
        for j in range(GROUP):
            if first:
                acc[j] = right_part(qd, j)
            else:
                acc[j] += right_part(qd, j)

    def grad_squares(qd, total):
        rows = block[qd, pl.ds(pl.multiple_of(m * QUARTER, QUARTER), QUARTER), :].astype(F32)
        return total + jnp.sum((rows * rows).reshape(QUARTER // 8, 8, 2, LANES), axis=(0, 2))

    total = jnp.zeros((8, LANES), F32)
    group_fwd(1, 2)
    group_fwd(1, 3)

    @pl.when(odd_z == 0)
    def _():
        pass_stop(mid_fwd, behind, stop_fwd, zf_s.at[8], stop_r.at[0], zf_r)

    forward_xy(quads[0])
    loads[1].wait()
    forward_xy(quads[1])
    share(quads[0])
    await_bytes(rroot.at[m_across], r_r.at[0])
    send_root(m_across, 2, sibling, range(4))
    forward_xy(quads[2])
    share(quads[1])
    forward_xy(quads[3])
    gather_chunk(quads[0])
    left_product(quads[0])
    total = grad_squares(quads[0], total)
    share(quads[2])
    gather_chunk(quads[1])
    left_product(quads[1])
    total = grad_squares(quads[1], total)
    await_bytes(rroot.at[0], r_r.at[1])
    await_bytes(rroot.at[0], r_r.at[2])
    right_product(quads[0], first=True)
    right_product(quads[1])
    share(quads[3])
    gather_chunk(quads[2])
    left_product(quads[2])
    total = grad_squares(quads[2], total)
    right_product(quads[2])
    gather_chunk(quads[3])
    left_product(quads[3])

    prec_total = jnp.zeros((8, LANES), F32)
    for c in range(4):
        value = (acc[c] + right_part(quads[3], c)).astype(BF16)
        for pair in range(2):
            rows = value[:, pair * LANES : (pair + 1) * LANES].reshape(NQ, 2, 16, LANES)
            even, odd = halves(rows[:, 0].reshape(LANES, LANES), rows[:, 1].reshape(LANES, LANES))
            send_back[c * 4 + 2 * pair] = even.reshape(NQ, 16, LANES)
            send_back[c * 4 + 2 * pair + 1] = odd.reshape(NQ, 16, LANES)
        wider = value.astype(F32)
        prec_total += jnp.sum((wider * wider).reshape(QUARTER // 8, 8, 2, LANES), axis=(0, 2))

    sums[m, 0] = grad_squares(quads[3], total)
    sums[m, 1] = prec_total
    for step in range(1, GROUP):
        fd = own_q * GROUP + (m + step) % GROUP
        remote(sums.at[m], sums.at[m], ex_s.at[step - 1], ex_r.at[m], z, fd).start()
    my_slot = by_parity(z)

    def hop_back(step):
        if step > 2:
            await_bytes(send_back.at[pl.ds(0, 2)], zb_s.at[step - 2])
        for sign in (1, -1):
            zd = (z + sign * step * way + NZ) % NZ
            remote(send_back.at[zd], mid_back.at[my_slot], zb_s.at[step], zb_r.at[my_slot], zd, f).start()

    opposite(send_back, stop_back, zb_s.at[0], stop_r.at[1])
    hop_back(1)
    hop_back(2)
    local(send_back.at[z], mid_back.at[my_slot], zb_r.at[my_slot]).start()
    for step in range(1, GROUP):
        await_bytes(sums.at[0], ex_r.at[(m + step) % GROUP])
    grad_sq = jnp.sum(sums[0, 0] + sums[1, 0] + sums[2, 0] + sums[3, 0], keepdims=True)
    prec_sq = jnp.sum(sums[0, 1] + sums[1, 1] + sums[2, 1] + sums[3, 1], keepdims=True)
    gains[z] = jnp.broadcast_to(jnp.sqrt((grad_sq + EPS) / (prec_sq + EPS)), (1, LANES))
    for step in range(1, NZ):
        zd = (z + step) % NZ
        remote(gains.at[z], gains.at[z], gain_s, gain_r.at[z], zd, f).start()
    hop_back(3)
    hop_back(4)
    pass_stop(mid_back, by_parity(behind), stop_back, zb_s.at[0], stop_r.at[1], zb_r)

    def back_xy(chunk, start=0, count=4):
        for t in range(count):
            slot = chunk * 4 + start + t
            plane = slot % 8 * 2 + slot // 8
            await_bytes(mid_back.at[slot], zb_r.at[slot])

            @pl.when(plane != z)
            def _():
                await_bytes(gains.at[plane], gain_r.at[plane])

            mid_back[slot] = (mid_back[slot].astype(F32) * gains[plane].reshape(1, 1, LANES)).astype(BF16)
        for i in range(NQ):
            d = (f % NQ + i) % NQ
            fd = m * NQ + d
            src = mid_back.at[pl.ds(chunk * 4 + start, count), d]
            dst = final.at[own_q, pl.ds(chunk * 4 + start, count)]
            if i > 0:
                remote(src, dst, xb_s.at[chunk], xb_r.at[chunk], z, fd).start()
                continue

            @pl.when(x != m)
            def _():
                remote(src, dst, xb_s.at[chunk], xb_r.at[chunk], z, fd).start()

            @pl.when(x == m)
            def _():
                local(src, dst, xb_r.at[chunk]).start()

    def gram_left():
        rows = pl.ds(pl.multiple_of(m * QUARTER, QUARTER), QUARTER)
        for j in range(GROUP):
            gram = jnp.zeros((QUARTER, QUARTER), F32)
            for c in range(4):
                gram += lax.dot_general(
                    block[c, rows, :], block[c, j * QUARTER : (j + 1) * QUARTER, :], NT, preferred_element_type=F32
                )
            cols = slice(j * QUARTER, (j + 1) * QUARTER)
            lnew[:, cols] = (BETA * lfac[:, cols].astype(F32) + (1.0 - BETA) / B * gram).astype(BF16)

    def gram_right():
        for j in range(GROUP):
            gram = lax.dot_general(block[m], block[j], TN, preferred_element_type=F32)
            cols = slice(j * QUARTER, (j + 1) * QUARTER)
            rnew[:, cols] = (BETA * rfac[:, cols].astype(F32) + (1.0 - BETA) / B * gram).astype(BF16)

    loads[3].wait()
    gram_left()
    stores = [local(lnew, ln_out, out_sem.at[0]), local(rnew, rn_out, out_sem.at[1])]
    stores[0].start()
    hop_back(5)
    hop_back(6)
    loads[4].wait()
    gram_right()
    stores[1].start()
    hop_back(7)
    half = z // 8
    back_xy(half)
    back_xy(1 - half)
    back_xy(2 + half)
    back_xy(3 - half, 0, 2)
    back_xy(3 - half, 2, 2)

    for chunk in range(4):
        await_bytes(final.at[:, pl.ds(chunk * 4, 4)], xb_r.at[chunk])

    await_bytes(stop_fwd, zf_s.at[8])
    for sem, paired in ((3, odd_z == 1), (7, odd_z == 0)):
        await_bytes(stop_fwd, zf_s.at[sem])

        @pl.when(paired)
        def _():
            await_bytes(stop_fwd, zf_s.at[sem])

    await_bytes(send_fwd.at[pl.ds(0, 2)], zf_s.at[6])
    for step in (0, 6, 7):
        await_bytes(send_back.at[pl.ds(0, 2)], zb_s.at[step])
    for c in range(4):
        await_bytes(raw.at[pl.ds(0, 15), 0, pl.ds(0, 4)], xf_s.at[c])
        await_bytes(raw.at[:, 0, pl.ds(0, 4)], sib_s.at[c])

        @pl.when(x == m)
        def _():
            await_bytes(final.at[pl.ds(0, NQ - 1), pl.ds(0, 4)], xb_s.at[c])

        @pl.when(x != m)
        def _():
            await_bytes(final.at[:, pl.ds(0, 4)], xb_s.at[c])

    await_bytes(gains.at[pl.ds(0, NZ - 1)], gain_s)
    for i in range(3):
        await_bytes(rroot.at[0], r_s.at[i])
        await_bytes(sums.at[0], ex_s.at[i])
    stores[0].wait()
    stores[1].wait()


def finish(owner_ref, final, lnew, rnew, dir_out, ln_out, rn_out, rows_in, wide, dirv, lvmem, rvmem, in_sem, out_sem):
    loads = [pltpu.make_async_copy(final.at[q], rows_in.at[q], in_sem.at[q]) for q in range(NQ)]
    stores = [
        pltpu.make_async_copy(lvmem, ln_out, out_sem.at[0]),
        pltpu.make_async_copy(rvmem, rn_out, out_sem.at[1]),
        pltpu.make_async_copy(dirv, dir_out, out_sem.at[2]),
    ]
    loads.append(pltpu.make_async_copy(lnew, lvmem, in_sem.at[NQ]))
    loads.append(pltpu.make_async_copy(rnew, rvmem, in_sem.at[NQ + 1]))
    for copy in loads:
        copy.start()
    row = lax.broadcasted_iota(jnp.int32, (LANES, LANES), 0)
    place_of = lax.rem(row, NZ)
    plane = lax.rem(place_of, NZ // 2) * 2 + lax.div(place_of, NZ // 2)
    slot_of = plane * NQ + lax.div(row, NZ)
    place = (jnp.broadcast_to(owner_ref[...], (LANES, LANES)) == slot_of).astype(BF16)
    for q in range(NQ):
        loads[q].wait()
        wide[q * 256 : q * 256 + 256, :] = rows_in[q].reshape(256, LANES).astype(F32)
    for i in range(2):
        loads[NQ + i].wait()
        stores[i].start()
    for t in range(16):
        rows = wide[pl.ds(t, LANES, stride=16), :].astype(BF16)
        blocks = lax.dot_general(rows, place, TN, preferred_element_type=F32).astype(BF16)
        dirv[t * 64 : t * 64 + 64, :] = blocks[:64]
        dirv[(16 + t) * 64 : (16 + t) * 64 + 64, :] = blocks[64:]
    stores[2].start()
    for copy in stores:
        copy.wait()


def per_device(gradient, owner_slot, left_factor, right_factor, left_root, right_root):
    blocks, row_width, col_width = gradient.shape
    columns = gradient.transpose(1, 2, 0).reshape(row_width * col_width, blocks)
    anywhere = pl.BlockSpec(memory_space=pl.ANY)
    factor = jax.ShapeDtypeStruct((QUARTER, B), BF16)
    dma = pltpu.SemaphoreType.DMA
    owner = owner_slot.reshape(1, blocks)
    final, left_new, right_new = pl.pallas_call(
        kernel,
        out_shape=(jax.ShapeDtypeStruct((NQ, NZ, 16, LANES), BF16), factor, factor),
        in_specs=[pl.BlockSpec(memory_space=pltpu.VMEM)] + [anywhere] * 5,
        out_specs=(anywhere, anywhere, anywhere),
        scratch_shapes=[
            pltpu.VMEM((2048, LANES), BF16),
            pltpu.VMEM((2048, LANES), F32),
            pltpu.VMEM((NZ, NQ, 16, LANES), BF16),
            pltpu.VMEM((NZ, NQ, 16, LANES), BF16),
            pltpu.VMEM((NF // 2, 2, NZ, 16, LANES), BF16),
            pltpu.VMEM((4, B, QUARTER), BF16),
            pltpu.VMEM((QUARTER, B), BF16),
            pltpu.VMEM((GROUP, QUARTER, B), BF16),
            pltpu.VMEM((QUARTER, B), BF16),
            pltpu.VMEM((QUARTER, B), BF16),
            pltpu.VMEM((4, QUARTER, QUARTER), BF16),
            pltpu.VMEM((GROUP, QUARTER, QUARTER), F32),
            pltpu.VMEM((NZ, 1, LANES), F32),
            pltpu.VMEM((GROUP, 2, 8, LANES), F32),
            pltpu.VMEM((NZ, NQ, 16, LANES), BF16),
            pltpu.VMEM((NZ, NQ, 16, LANES), BF16),
            pltpu.VMEM((QUARTER, B), BF16),
            pltpu.VMEM((QUARTER, B), BF16),
            pltpu.VMEM((NQ, 16, LANES), BF16),
            pltpu.VMEM((NQ, 16, LANES), BF16),
            dma((5,)), dma((2,)),
            dma((9,)), dma((NZ,)),
            dma((4,)), dma((4, 4)),
            dma((4,)), dma((4,)),
            dma((3,)), dma((3,)),
            dma((3,)), dma((GROUP,)),
            dma, dma((NZ,)),
            dma((8,)), dma((NZ,)),
            dma((4,)), dma((4,)),
            dma((2,)),
        ],
        compiler_params=pltpu.CompilerParams(
            collective_id=0, has_side_effects=True, vmem_limit_bytes=60 * 1024 * 1024
        ),
        cost_estimate=pl.CostEstimate(flops=2_200_000_000, bytes_accessed=8_000_000, transcendentals=0),
    )(owner, columns, left_factor, right_factor, left_root, right_root)
    direction, left_new, right_new = pl.pallas_call(
        finish,
        out_shape=(jax.ShapeDtypeStruct(columns.shape, BF16), factor, factor),
        in_specs=[pl.BlockSpec(memory_space=pltpu.VMEM)] + [anywhere] * 3,
        out_specs=(anywhere, anywhere, anywhere),
        scratch_shapes=[
            pltpu.VMEM((NQ, NZ, 16, LANES), BF16),
            pltpu.VMEM((2048, LANES), F32),
            pltpu.VMEM((2048, LANES), BF16),
            pltpu.VMEM((QUARTER, B), BF16),
            pltpu.VMEM((QUARTER, B), BF16),
            dma((NQ + 2,)),
            dma((3,)),
        ],
        compiler_params=pltpu.CompilerParams(vmem_limit_bytes=60 * 1024 * 1024),
        cost_estimate=pl.CostEstimate(flops=70_000_000, bytes_accessed=4_000_000, transcendentals=0),
    )(owner, final, left_new, right_new)
    return direction.reshape(row_width, col_width, blocks).transpose(2, 0, 1), left_new, right_new


def solution(mesh):
    placed = (
        P(None, "fsdp", "rep"),
        P(),
        P(("rep", "fsdp"), None),
        P(("rep", "fsdp"), None),
        P(("rep", "fsdp"), None),
        P(("rep", "fsdp"), None),
    )
    return jax.shard_map(
        per_device,
        mesh=mesh,
        in_specs=placed,
        out_specs=(P(None, "fsdp", "rep"), P(("rep", "fsdp"), None), P(("rep", "fsdp"), None)),
        check_vma=False,
    )
```

```python
import functools

import jax
import jax.numpy as jnp
from jax import lax
from jax.experimental import pallas as pl
from jax.experimental.pallas import tpu as pltpu
from jax.sharding import PartitionSpec as P

MESH = pl.DeviceIdType.MESH
F32 = jnp.float32
BF16 = jnp.bfloat16
B = 1024
GROUP = 4
BETA = 0.9
EPS = 1e-06
NZ = 16
NF = 32
NQ = NF // GROUP
QUARTER = B // GROUP
LANES = 128
NT = (((1,), (1,)), ((), ()))
TN = (((0,), (0,)), ((), ()))
def halves(even, odd):
    lane = lax.broadcasted_iota(jnp.int32, even.shape, even.ndim - 1)
    low = lane < LANES // 2
    axis = even.ndim - 1
    top = jnp.where(low, even, pltpu.roll(odd, LANES // 2, axis))
    bottom = jnp.where(low, pltpu.roll(even, LANES // 2, axis), odd)
    return top, bottom


def kernel(
    owner_ref, grad_in, lf_in, rf_in, lr_in, rr_in,
    final, ln_out, rn_out,
    grad, wide, send_fwd, mid_fwd, raw, block, lroot, rroot, lfac, rfac,
    tpart, acc, gains, sums, send_back, mid_back, lnew, rnew, stop_fwd, stop_back,
    in_sem, out_sem, zf_s, zf_r, xf_s, xf_r, sib_s, sib_r, r_s, r_r,
    ex_s, ex_r, gain_s, gain_r, zb_s, zb_r, xb_s, xb_r, stop_r,
):
    z = lax.axis_index("rep")
    f = lax.axis_index("fsdp")
    core = f % 2
    xy = f // 2
    m = f % GROUP
    own_q = f // GROUP
    x = f // 8
    zq = z // 4
    sibling = f + 1 - 2 * core
    across = f + 2 - 4 * (m // 2)
    m_across = m + 2 - 4 * (m // 2)
    near = 1 + 2 * (1 - (z % 4) // 2)
    quads = [zq, (zq + near) % 4, (zq + 4 - near) % 4, (zq + 2) % 4]

    def local(src, dst, sem):
        return pltpu.make_async_copy(src, dst, sem)

    def remote(src, dst, send, recv, zd, fd):
        return pltpu.make_async_remote_copy(
            src_ref=src, dst_ref=dst, send_sem=send, recv_sem=recv,
            device_id=(zd, fd), device_id_type=MESH,
        )

    def await_bytes(ref, sem):
        pltpu.make_async_copy(ref, ref, sem).wait()

    loads = [
        local(grad_in, grad, in_sem.at[0]),
        local(lr_in, lroot.at[core], in_sem.at[1]),
        local(rr_in, rroot.at[0], in_sem.at[2]),
        local(lf_in, lfac, in_sem.at[3]),
        local(rf_in, rfac, in_sem.at[4]),
    ]
    for load in loads:
        load.start()
    barrier = pltpu.get_barrier_semaphore()

    def greet_plane(i, carry):
        pl.semaphore_signal(barrier, inc=1, device_id=(z, (f + i) % NF), device_id_type=MESH)
        return carry

    def greet_ring(i, carry):
        pl.semaphore_signal(barrier, inc=1, device_id=((z + i) % NZ, f), device_id_type=MESH)
        return carry

    def greet_senders(i, carry):
        pl.semaphore_signal(barrier, inc=1, device_id=((z + i) % NZ, sibling), device_id_type=MESH)
        return carry

    lax.fori_loop(1, NZ, greet_ring, 0)
    lax.fori_loop(1, NF, greet_plane, 0)
    lax.fori_loop(1, NZ, greet_senders, 0)

    owner = owner_ref[...]
    slot_row = lax.broadcasted_iota(jnp.int32, (LANES, LANES), 0)
    pick = (jnp.broadcast_to(owner, (LANES, LANES)) == slot_row).astype(BF16)
    loads[0].wait()
    for t in range(16):
        piece = jnp.concatenate((grad[t * 64 : t * 64 + 64, :], grad[(16 + t) * 64 : (16 + t) * 64 + 64, :]), axis=0)
        wide[pl.ds(t, LANES, stride=16), :] = lax.dot_general(pick, piece, NT, preferred_element_type=F32)
    for zd in range(NZ):
        send_fwd[zd] = wide[zd * 128 : zd * 128 + 128, :].reshape(NQ, 16, LANES).astype(BF16)

    pl.semaphore_wait(barrier, 2 * (NZ - 1) + NF - 1)

    way = 1 - 2 * core

    def send_z(send, mid, send_sem, recv_sem, step):
        zd = (z + step * way + NZ) % NZ
        remote(send.at[zd], mid.at[z], send_sem, recv_sem.at[z], zd, f).start()

    def send_stop(send, stop, send_sem, recv_sem):
        zd = (z + way + NZ) % NZ
        remote(send.at[(z + NZ // 2) % NZ], stop, send_sem, recv_sem, zd, f).start()

    def pass_stop(mid, stop, send_sem, stop_sem, recv_sem):
        await_bytes(stop, stop_sem)
        origin = (z - way + NZ) % NZ
        zd = (z + 7 * way + NZ) % NZ
        remote(stop, mid.at[origin], send_sem, recv_sem.at[origin], zd, f).start()

    def send_right(part):
        rows = pl.ds(part * 64, 64)
        remote(rroot.at[0, rows], rroot.at[1, rows], r_s.at[0], r_r.at[0], z, across).start()

    def send_left(part):
        rows = lroot.at[core, pl.ds(part * 64, 64)]
        remote(rows, rows, r_s.at[1], r_r.at[1], z, sibling).start()

    loads[1].wait()
    loads[2].wait()
    send_stop(send_fwd, stop_fwd, zf_s, stop_r.at[0])
    for step in range(1, 6):
        for sign in (1, -1):
            send_z(send_fwd, mid_fwd, zf_s, zf_r, sign * step)
        if step < 5:
            send_right(step - 1)
            send_left(step - 1)
    local(send_fwd.at[z], mid_fwd.at[z], zf_r.at[z]).start()
    pass_stop(mid_fwd, stop_fwd, zf_s, stop_r.at[0], zf_r)

    def forward_xy(qd):
        for t in range(4):
            await_bytes(mid_fwd.at[qd * 4 + t], zf_r.at[qd * 4 + t])

        for i in range(NF // 2):
            chip = (xy + i) % (NF // 2)
            q = chip // 2
            src = mid_fwd.at[pl.ds(qd * 4, 4), q]
            dst = raw.at[xy, core, pl.ds(qd * 4, 4)]
            if i == 0:
                local(src, dst, xf_r.at[qd, x]).start()
            else:
                remote(src, dst, xf_s.at[qd], xf_r.at[qd, x], z, chip * 2 + core).start()

    def share(qd):
        for i in range(4):
            column = (x + i) % 4
            mine = raw.at[pl.ds(column * 4, 4), core, pl.ds(qd * 4, 4)]
            await_bytes(mine, xf_r.at[qd, column])
            remote(mine, mine, sib_s.at[qd], sib_r.at[qd], z, sibling).start()

    def gather_chunk(qd):
        await_bytes(raw.at[:, 1 - core, pl.ds(qd * 4, 4)], sib_r.at[qd])

        def unpack(i, carry):
            for pair in range(2):
                first = qd * 4 + 2 * pair
                even = raw[pl.ds(i * 2, 2), :, first].reshape(64, LANES)
                odd = raw[pl.ds(i * 2, 2), :, first + 1].reshape(64, LANES)
                top, bottom = halves(even, odd)
                rows = jnp.concatenate((top.reshape(4, 16, LANES), bottom.reshape(4, 16, LANES)), axis=1)
                at = pl.multiple_of(i * 128, 128)
                block[qd, pl.ds(at, 128), pair * LANES : (pair + 1) * LANES] = rows.reshape(128, LANES)
            return carry

        lax.fori_loop(0, NF // 4, unpack, 0)

    def left_product(qd):
        for k in range(2):
            tpart[k, qd] = jnp.dot(lroot[k], block[qd], preferred_element_type=F32).astype(BF16)

    def right_part(qd, k, j):
        return lax.dot_general(
            tpart[k, qd], rroot[j, :, pl.ds(pl.multiple_of(qd * QUARTER, QUARTER), QUARTER)], NT,
            preferred_element_type=F32,
        )

    def right_product(qd, first=False):
        for k in range(2):
            for j in range(2):
                if first:
                    acc[2 * k + j] = right_part(qd, k, j)
                else:
                    acc[2 * k + j] += right_part(qd, k, j)

    def grad_squares(qd, total):
        rows = block[qd, pl.ds(pl.multiple_of(m * QUARTER, QUARTER), QUARTER), :].astype(F32)
        return total + jnp.sum((rows * rows).reshape(QUARTER // 8, 8, 2, LANES), axis=(0, 2))

    total = jnp.zeros((8, LANES), F32)
    forward_xy(quads[0])
    for step in (6, 7):
        for sign in (1, -1):
            send_z(send_fwd, mid_fwd, zf_s, zf_r, sign * step)
    forward_xy(quads[1])
    share(quads[0])
    forward_xy(quads[2])
    share(quads[1])
    gather_chunk(quads[0])
    await_bytes(lroot.at[0], r_r.at[1])
    left_product(quads[0])
    total = grad_squares(quads[0], total)
    forward_xy(quads[3])
    share(quads[2])
    gather_chunk(quads[1])
    left_product(quads[1])
    total = grad_squares(quads[1], total)
    await_bytes(rroot.at[1], r_r.at[0])
    right_product(quads[0], first=True)
    right_product(quads[1])
    share(quads[3])
    gather_chunk(quads[2])
    left_product(quads[2])
    total = grad_squares(quads[2], total)
    right_product(quads[2])
    gather_chunk(quads[3])
    left_product(quads[3])

    prec_total = jnp.zeros((8, LANES), F32)
    for k in range(2):
        for j in range(2):
            value = (acc[2 * k + j] + right_part(quads[3], k, j)).astype(BF16)
            for pair in range(2):
                rows = value[:, pair * LANES : (pair + 1) * LANES].reshape(NQ, 2, 16, LANES)
                even, odd = halves(rows[:, 0].reshape(LANES, LANES), rows[:, 1].reshape(LANES, LANES))
                send_back[k, j, 2 * pair] = even.reshape(NQ, 16, LANES)
                send_back[k, j, 2 * pair + 1] = odd.reshape(NQ, 16, LANES)
            wider = value.astype(F32)
            prec_total += jnp.sum((wider * wider).reshape(QUARTER // 8, 8, 2, LANES), axis=(0, 2))

    sums[m, 0] = grad_squares(quads[3], total)
    sums[m, 1] = prec_total
    for step in range(1, GROUP):
        fd = own_q * GROUP + (m + step) % GROUP
        remote(sums.at[m], sums.at[m], ex_s.at[step - 1], ex_r.at[m], z, fd).start()
    def send_rows(k, j, t):
        piece = send_back.at[k, j, t]
        zd = (m if j == 0 else m_across) * 4 + t
        fd = f - core + k
        here = zd == z

        @pl.when(here & (core == k))
        def _():
            local(piece, mid_back.at[z], zb_r.at[z]).start()

        @pl.when(here & (core != k))
        def _():
            remote(piece, mid_back.at[z], zb_s, zb_r.at[z], z, sibling).start()

        far = zd == (z + NZ // 2) % NZ

        @pl.when(far)
        def _():
            remote(piece, stop_back, zb_s, stop_r.at[1], (z + NZ + 1 - 2 * k) % NZ, fd).start()

        @pl.when(jnp.logical_not(here | far))
        def _():
            remote(piece, mid_back.at[z], zb_s, zb_r.at[z], zd, fd).start()

    for t in range(2):
        for j in range(2):
            for k in range(2):
                send_rows(k, j, t)
    for step in range(1, GROUP):
        await_bytes(sums.at[0], ex_r.at[(m + step) % GROUP])
    grad_sq = jnp.sum(sums[0, 0] + sums[1, 0] + sums[2, 0] + sums[3, 0], keepdims=True)
    prec_sq = jnp.sum(sums[0, 1] + sums[1, 1] + sums[2, 1] + sums[3, 1], keepdims=True)
    gains[z] = jnp.broadcast_to(jnp.sqrt((grad_sq + EPS) / (prec_sq + EPS)), (1, LANES))
    for step in range(1, NZ):
        zd = (z + step) % NZ
        remote(gains.at[z], gains.at[z], gain_s, gain_r.at[z], zd, f).start()
    for t in range(2, 4):
        for j in range(2):
            for k in range(2):
                send_rows(k, j, t)
    pass_stop(mid_back, stop_back, zb_s, stop_r.at[1], zb_r)

    def back_xy(qd):
        for t in range(4):
            zs = qd * 4 + t
            await_bytes(mid_back.at[zs], zb_r.at[zs])

            @pl.when(zs != z)
            def _():
                await_bytes(gains.at[zs], gain_r.at[zs])

            mid_back[zs] = (mid_back[zs].astype(F32) * gains[zs].reshape(1, 1, LANES)).astype(BF16)
        for i in range(NQ):
            d = (f % NQ + i) % NQ
            fd = m * NQ + d
            src = mid_back.at[pl.ds(qd * 4, 4), d]
            dst = final.at[own_q, pl.ds(qd * 4, 4)]
            if i > 0:
                remote(src, dst, xb_s.at[qd], xb_r.at[qd], z, fd).start()
                continue

            @pl.when(x != m)
            def _():
                remote(src, dst, xb_s.at[qd], xb_r.at[qd], z, fd).start()

            @pl.when(x == m)
            def _():
                local(src, dst, xb_r.at[qd]).start()

    def gram_left():
        rows = pl.ds(pl.multiple_of(m * QUARTER, QUARTER), QUARTER)
        for j in range(GROUP):
            gram = jnp.zeros((QUARTER, QUARTER), F32)
            for c in range(4):
                gram += lax.dot_general(
                    block[c, rows, :], block[c, j * QUARTER : (j + 1) * QUARTER, :], NT, preferred_element_type=F32
                )
            cols = slice(j * QUARTER, (j + 1) * QUARTER)
            lnew[:, cols] = (BETA * lfac[:, cols].astype(F32) + (1.0 - BETA) / B * gram).astype(BF16)

    def gram_right():
        for j in range(GROUP):
            gram = lax.dot_general(block[m], block[j], TN, preferred_element_type=F32)
            cols = slice(j * QUARTER, (j + 1) * QUARTER)
            rnew[:, cols] = (BETA * rfac[:, cols].astype(F32) + (1.0 - BETA) / B * gram).astype(BF16)

    loads[3].wait()
    gram_left()
    stores = [local(lnew, ln_out, out_sem.at[0]), local(rnew, rn_out, out_sem.at[1])]
    stores[0].start()
    back_xy(quads[0])
    loads[4].wait()
    gram_right()
    stores[1].start()
    back_xy(quads[1])
    back_xy(quads[2])
    back_xy(quads[3])

    for qd in quads:
        await_bytes(final.at[:, pl.ds(qd * 4, 4)], xb_r.at[qd])

    await_bytes(send_fwd, zf_s)
    await_bytes(send_fwd, zb_s)

    @pl.when(zq % 2 != core)
    def _():
        await_bytes(stop_back, zb_s)

    for c in range(4):
        await_bytes(raw.at[pl.ds(0, 15), 0, pl.ds(0, 4)], xf_s.at[c])
        await_bytes(raw.at[:, 0, pl.ds(0, 4)], sib_s.at[c])

        @pl.when(x == m)
        def _():
            await_bytes(final.at[pl.ds(0, NQ - 1), pl.ds(0, 4)], xb_s.at[c])

        @pl.when(x != m)
        def _():
            await_bytes(final.at[:, pl.ds(0, 4)], xb_s.at[c])

    await_bytes(gains.at[pl.ds(0, NZ - 1)], gain_s)
    for i in range(2):
        await_bytes(rroot.at[0], r_s.at[i])
    for i in range(3):
        await_bytes(sums.at[0], ex_s.at[i])
    stores[0].wait()
    stores[1].wait()


def finish(owner_ref, final, lnew, rnew, dir_out, ln_out, rn_out, rows_in, wide, dirv, lvmem, rvmem, in_sem, out_sem):
    loads = [pltpu.make_async_copy(final.at[q], rows_in.at[q], in_sem.at[q]) for q in range(NQ)]
    stores = [
        pltpu.make_async_copy(lvmem, ln_out, out_sem.at[0]),
        pltpu.make_async_copy(rvmem, rn_out, out_sem.at[1]),
        pltpu.make_async_copy(dirv, dir_out, out_sem.at[2]),
    ]
    loads.append(pltpu.make_async_copy(lnew, lvmem, in_sem.at[NQ]))
    loads.append(pltpu.make_async_copy(rnew, rvmem, in_sem.at[NQ + 1]))
    for copy in loads:
        copy.start()
    row = lax.broadcasted_iota(jnp.int32, (LANES, LANES), 0)
    slot_of = (row % NZ) * NQ + row // NZ
    place = (jnp.broadcast_to(owner_ref[...], (LANES, LANES)) == slot_of).astype(BF16)
    for q in range(NQ):
        loads[q].wait()
        wide[q * 256 : q * 256 + 256, :] = rows_in[q].reshape(256, LANES).astype(F32)
    for i in range(2):
        loads[NQ + i].wait()
        stores[i].start()
    for t in range(16):
        rows = wide[pl.ds(t, LANES, stride=16), :].astype(BF16)
        blocks = lax.dot_general(rows, place, TN, preferred_element_type=F32).astype(BF16)
        dirv[t * 64 : t * 64 + 64, :] = blocks[:64]
        dirv[(16 + t) * 64 : (16 + t) * 64 + 64, :] = blocks[64:]
    stores[2].start()
    for copy in stores:
        copy.wait()


def per_device(gradient, owner_slot, left_factor, right_factor, left_root, right_root):
    blocks, row_width, col_width = gradient.shape
    columns = gradient.transpose(1, 2, 0).reshape(row_width * col_width, blocks)
    anywhere = pl.BlockSpec(memory_space=pl.ANY)
    factor = jax.ShapeDtypeStruct((QUARTER, B), BF16)
    dma = pltpu.SemaphoreType.DMA
    owner = owner_slot.reshape(1, blocks)
    final, left_new, right_new = pl.pallas_call(
        kernel,
        out_shape=(jax.ShapeDtypeStruct((NQ, NZ, 16, LANES), BF16), factor, factor),
        in_specs=[pl.BlockSpec(memory_space=pltpu.VMEM)] + [anywhere] * 5,
        out_specs=(anywhere, anywhere, anywhere),
        scratch_shapes=[
            pltpu.VMEM((2048, LANES), BF16),
            pltpu.VMEM((2048, LANES), F32),
            pltpu.VMEM((NZ, NQ, 16, LANES), BF16),
            pltpu.VMEM((NZ, NQ, 16, LANES), BF16),
            pltpu.VMEM((NF // 2, 2, NZ, 16, LANES), BF16),
            pltpu.VMEM((4, B, QUARTER), BF16),
            pltpu.VMEM((2, QUARTER, B), BF16),
            pltpu.VMEM((2, QUARTER, B), BF16),
            pltpu.VMEM((QUARTER, B), BF16),
            pltpu.VMEM((QUARTER, B), BF16),
            pltpu.VMEM((2, 4, QUARTER, QUARTER), BF16),
            pltpu.VMEM((GROUP, QUARTER, QUARTER), F32),
            pltpu.VMEM((NZ, 1, LANES), F32),
            pltpu.VMEM((GROUP, 2, 8, LANES), F32),
            pltpu.VMEM((2, 2, 4, NQ, 16, LANES), BF16),
            pltpu.VMEM((NZ, NQ, 16, LANES), BF16),
            pltpu.VMEM((QUARTER, B), BF16),
            pltpu.VMEM((QUARTER, B), BF16),
            pltpu.VMEM((NQ, 16, LANES), BF16),
            pltpu.VMEM((NQ, 16, LANES), BF16),
            dma((5,)), dma((2,)),
            dma, dma((NZ,)),
            dma((4,)), dma((4, 4)),
            dma((4,)), dma((4,)),
            dma((2,)), dma((2,)),
            dma((3,)), dma((GROUP,)),
            dma, dma((NZ,)),
            dma, dma((NZ,)),
            dma((4,)), dma((4,)),
            dma((2,)),
        ],
        compiler_params=pltpu.CompilerParams(
            collective_id=0, has_side_effects=True, vmem_limit_bytes=60 * 1024 * 1024
        ),
        cost_estimate=pl.CostEstimate(flops=2_200_000_000, bytes_accessed=8_000_000, transcendentals=0),
    )(owner, columns, left_factor, right_factor, left_root, right_root)
    direction, left_new, right_new = pl.pallas_call(
        finish,
        out_shape=(jax.ShapeDtypeStruct(columns.shape, BF16), factor, factor),
        in_specs=[pl.BlockSpec(memory_space=pltpu.VMEM)] + [anywhere] * 3,
        out_specs=(anywhere, anywhere, anywhere),
        scratch_shapes=[
            pltpu.VMEM((NQ, NZ, 16, LANES), BF16),
            pltpu.VMEM((2048, LANES), F32),
            pltpu.VMEM((2048, LANES), BF16),
            pltpu.VMEM((QUARTER, B), BF16),
            pltpu.VMEM((QUARTER, B), BF16),
            dma((NQ + 2,)),
            dma((3,)),
        ],
        compiler_params=pltpu.CompilerParams(vmem_limit_bytes=60 * 1024 * 1024),
        cost_estimate=pl.CostEstimate(flops=70_000_000, bytes_accessed=4_000_000, transcendentals=0),
    )(owner, final, left_new, right_new)
    return direction.reshape(row_width, col_width, blocks).transpose(2, 0, 1), left_new, right_new


def solution(mesh):
    placed = (
        P(None, "fsdp", "rep"),
        P(),
        P(("rep", "fsdp"), None),
        P(("rep", "fsdp"), None),
        P(("rep", "fsdp"), None),
        P(("rep", "fsdp"), None),
    )
    return jax.shard_map(
        per_device,
        mesh=mesh,
        in_specs=placed,
        out_specs=(P(None, "fsdp", "rep"), P(("rep", "fsdp"), None), P(("rep", "fsdp"), None)),
        check_vma=False,
    )
```

```python
import functools

import jax
import jax.numpy as jnp
from jax import lax
from jax.experimental import pallas as pl
from jax.experimental.pallas import tpu as pltpu
from jax.sharding import PartitionSpec as P

MESH = pl.DeviceIdType.MESH
F32 = jnp.float32
BF16 = jnp.bfloat16
B = 1024
GROUP = 4
BETA = 0.9
EPS = 1e-06
NZ = 16
NF = 32
NQ = NF // GROUP
QUARTER = B // GROUP
LANES = 128
NT = (((1,), (1,)), ((), ()))
TN = (((0,), (0,)), ((), ()))
def halves(even, odd):
    lane = lax.broadcasted_iota(jnp.int32, even.shape, even.ndim - 1)
    low = lane < LANES // 2
    axis = even.ndim - 1
    top = jnp.where(low, even, pltpu.roll(odd, LANES // 2, axis))
    bottom = jnp.where(low, pltpu.roll(even, LANES // 2, axis), odd)
    return top, bottom


def kernel(
    owner_ref, grad_in, lf_in, rf_in, lr_in, rr_in,
    final, ln_out, rn_out,
    grad, wide, send_fwd, mid_fwd, raw, block, lroot, rroot, lfac, rfac,
    tpart, acc, gains, sums, send_back, mid_back, lnew, rnew, stop_fwd, stop_back,
    in_sem, out_sem, zf_s, zf_r, xf_s, xf_r, sib_s, sib_r, r_s, r_r,
    ex_s, ex_r, gain_s, gain_r, zb_s, zb_r, xb_s, xb_r, stop_r,
):
    z = lax.axis_index("rep")
    f = lax.axis_index("fsdp")
    core = f % 2
    xy = f // 2
    m = f % GROUP
    own_q = f // GROUP
    x = f // 8
    zq = z // 4
    sibling = f + 1 - 2 * core
    across = f + 2 - 4 * (m // 2)
    m_across = m + 2 - 4 * (m // 2)
    early = 2 * (1 - (z % 4) // 2)
    near = 1 + 2 * (1 - (z % 4) // 2)
    quads = [zq, (zq + near) % 4, (zq + 4 - near) % 4, (zq + 2) % 4]

    def local(src, dst, sem):
        return pltpu.make_async_copy(src, dst, sem)

    def remote(src, dst, send, recv, zd, fd):
        return pltpu.make_async_remote_copy(
            src_ref=src, dst_ref=dst, send_sem=send, recv_sem=recv,
            device_id=(zd, fd), device_id_type=MESH,
        )

    def await_bytes(ref, sem):
        pltpu.make_async_copy(ref, ref, sem).wait()

    loads = [
        local(grad_in, grad, in_sem.at[0]),
        local(lr_in, lroot, in_sem.at[1]),
        local(rr_in, rroot.at[m], in_sem.at[2]),
        local(lf_in, lfac, in_sem.at[3]),
        local(rf_in, rfac, in_sem.at[4]),
    ]
    for load in loads:
        load.start()
    barrier = pltpu.get_barrier_semaphore()

    def greet_plane(i, carry):
        pl.semaphore_signal(barrier, inc=1, device_id=(z, (f + i) % NF), device_id_type=MESH)
        return carry

    def greet_ring(i, carry):
        pl.semaphore_signal(barrier, inc=1, device_id=((z + i) % NZ, f), device_id_type=MESH)
        return carry

    lax.fori_loop(1, NZ, greet_ring, 0)
    lax.fori_loop(1, NF, greet_plane, 0)

    owner = owner_ref[...]
    slot_row = lax.broadcasted_iota(jnp.int32, (LANES, LANES), 0)
    pick = (jnp.broadcast_to(owner, (LANES, LANES)) == slot_row).astype(BF16)
    loads[0].wait()
    for t in range(0, 16, 2):
        starts = (t, 16 + t, t + 1, 17 + t)
        piece = jnp.concatenate([grad[r * 64 : r * 64 + 64, :] for r in starts], axis=0)
        tiles = lax.dot_general(pick, piece, NT, preferred_element_type=F32)
        wide[pl.ds(t, LANES, stride=16), :] = tiles[:, :LANES]
        wide[pl.ds(t + 1, LANES, stride=16), :] = tiles[:, LANES:]
    for zd in range(NZ):
        send_fwd[zd] = wide[zd * 128 : zd * 128 + 128, :].reshape(NQ, 16, LANES).astype(BF16)

    pl.semaphore_wait(barrier, NZ - 1 + NF - 1)

    way = 1 - 2 * core

    def send_z(send, mid, send_sem, recv_sem, step):
        zd = (z + step * way + NZ) % NZ
        remote(send.at[zd], mid.at[z], send_sem, recv_sem.at[z], zd, f).start()

    def send_stop(send, stop, send_sem, recv_sem):
        zd = (z + way + NZ) % NZ
        remote(send.at[(z + NZ // 2) % NZ], stop, send_sem, recv_sem, zd, f).start()

    def pass_stop(mid, stop, send_sem, stop_sem, recv_sem):
        await_bytes(stop, stop_sem)
        origin = (z - way + NZ) % NZ
        zd = (z + 7 * way + NZ) % NZ
        remote(stop, mid.at[origin], send_sem, recv_sem.at[origin], zd, f).start()

    def send_root(member, index, fd, parts):
        for part in parts:
            rows = rroot.at[member, pl.ds(part * 64, 64)]
            remote(rows, rows, r_s.at[index], r_r.at[index], z, fd).start()

    loads[2].wait()
    send_stop(send_fwd, stop_fwd, zf_s, stop_r.at[0])
    for step in range(1, 6):
        for sign in (1, -1):
            send_z(send_fwd, mid_fwd, zf_s, zf_r, sign * step)
        if step < 5:
            send_root(m, 0, across, (step - 1,))
    local(send_fwd.at[z], mid_fwd.at[z], zf_r.at[z]).start()
    send_root(m, 1, sibling, range(4))
    pass_stop(mid_fwd, stop_fwd, zf_s, stop_r.at[0], zf_r)

    def forward_xy(qd, start=0, count=4):
        for t in range(count):
            zs = qd * 4 + start + t
            await_bytes(mid_fwd.at[zs], zf_r.at[zs])
        sources = pl.ds(qd * 4 + start, count)

        for i in range(NF // 2):
            chip = (xy + i) % (NF // 2)
            q = chip // 2
            src = mid_fwd.at[sources, q]
            dst = raw.at[xy, core, sources]
            if i == 0:
                local(src, dst, xf_r.at[qd, x]).start()
            else:
                remote(src, dst, xf_s.at[qd], xf_r.at[qd, x], z, chip * 2 + core).start()

    def share(qd):
        for i in range(4):
            column = (x + i) % 4
            mine = raw.at[pl.ds(column * 4, 4), core, pl.ds(qd * 4, 4)]
            await_bytes(mine, xf_r.at[qd, column])
            remote(mine, mine, sib_s.at[qd], sib_r.at[qd], z, sibling).start()

    def gather_chunk(qd):
        await_bytes(raw.at[:, 1 - core, pl.ds(qd * 4, 4)], sib_r.at[qd])

        def unpack(i, carry):
            for pair in range(2):
                first = qd * 4 + 2 * pair
                even = raw[pl.ds(i * 4, 4), :, first].reshape(128, LANES)
                odd = raw[pl.ds(i * 4, 4), :, first + 1].reshape(128, LANES)
                top, bottom = halves(even, odd)
                rows = jnp.concatenate((top.reshape(8, 16, LANES), bottom.reshape(8, 16, LANES)), axis=1)
                at = pl.multiple_of(i * 256, 256)
                block[qd, pl.ds(at, 256), pair * LANES : (pair + 1) * LANES] = rows.reshape(256, LANES)
            return carry

        lax.fori_loop(0, NF // 8, unpack, 0)

    def left_product(qd):
        tpart[qd] = jnp.dot(lroot[...], block[qd], preferred_element_type=F32).astype(BF16)

    def right_part(qd, j):
        return lax.dot_general(
            tpart[qd], rroot[j, :, pl.ds(pl.multiple_of(qd * QUARTER, QUARTER), QUARTER)], NT,
            preferred_element_type=F32,
        )

    def right_product(qd, first=False):
        for j in range(GROUP):
            if first:
                acc[j] = right_part(qd, j)
            else:
                acc[j] += right_part(qd, j)

    def grad_squares(qd, total):
        rows = block[qd, pl.ds(pl.multiple_of(m * QUARTER, QUARTER), QUARTER), :].astype(F32)
        return total + jnp.sum((rows * rows).reshape(QUARTER // 8, 8, 2, LANES), axis=(0, 2))

    total = jnp.zeros((8, LANES), F32)
    forward_xy(quads[0])
    for step in (6, 7):
        for sign in (1, -1):
            send_z(send_fwd, mid_fwd, zf_s, zf_r, sign * step)
    forward_xy(quads[1])
    loads[1].wait()
    share(quads[0])
    forward_xy(quads[2])
    share(quads[1])
    forward_xy(quads[3], early, 2)
    gather_chunk(quads[0])
    left_product(quads[0])
    total = grad_squares(quads[0], total)
    await_bytes(rroot.at[m_across], r_r.at[0])
    send_root(m_across, 2, sibling, range(4))
    forward_xy(quads[3], 2 - early, 2)
    share(quads[2])
    gather_chunk(quads[1])
    left_product(quads[1])
    total = grad_squares(quads[1], total)
    await_bytes(rroot.at[0], r_r.at[1])
    await_bytes(rroot.at[0], r_r.at[2])
    right_product(quads[0], first=True)
    right_product(quads[1])
    share(quads[3])
    gather_chunk(quads[2])
    left_product(quads[2])
    total = grad_squares(quads[2], total)
    right_product(quads[2])
    gather_chunk(quads[3])
    left_product(quads[3])

    def last_product(qd):
        value = (acc[qd] + right_part(quads[3], qd)).astype(BF16)
        for pair in range(2):
            rows = value[:, pair * LANES : (pair + 1) * LANES].reshape(NQ, 2, 16, LANES)
            even, odd = halves(rows[:, 0].reshape(LANES, LANES), rows[:, 1].reshape(LANES, LANES))
            send_back[qd * 4 + 2 * pair] = even.reshape(NQ, 16, LANES)
            send_back[qd * 4 + 2 * pair + 1] = odd.reshape(NQ, 16, LANES)
        wider = value.astype(F32)
        return jnp.sum((wider * wider).reshape(QUARTER // 8, 8, 2, LANES), axis=(0, 2))

    def send_quad(qd, skip=None):
        for t in range(4):
            zd = qd * 4 + t

            def start():
                remote(send_back.at[zd], mid_back.at[z], zb_s, zb_r.at[z], zd, f).start()

            if skip is None:
                start()
            else:
                pl.when(zd != skip)(start)

    prec_total = last_product(quads[0])
    send_quad(quads[0], skip=z)
    local(send_back.at[z], mid_back.at[z], zb_r.at[z]).start()
    prec_total += last_product(quads[1])
    send_quad(quads[1])
    prec_total += last_product(quads[2])
    prec_total += last_product(quads[3])

    sums[m, 0] = grad_squares(quads[3], total)
    sums[m, 1] = prec_total
    for step in range(1, GROUP):
        fd = own_q * GROUP + (m + step) % GROUP
        remote(sums.at[m], sums.at[m], ex_s.at[step - 1], ex_r.at[m], z, fd).start()
    send_stop(send_back, stop_back, zb_s, stop_r.at[1])
    send_quad(quads[2])
    for step in range(1, GROUP):
        await_bytes(sums.at[0], ex_r.at[(m + step) % GROUP])
    grad_sq = jnp.sum(sums[0, 0] + sums[1, 0] + sums[2, 0] + sums[3, 0], keepdims=True)
    prec_sq = jnp.sum(sums[0, 1] + sums[1, 1] + sums[2, 1] + sums[3, 1], keepdims=True)
    gains[z] = jnp.broadcast_to(jnp.sqrt((grad_sq + EPS) / (prec_sq + EPS)), (1, LANES))
    for step in range(1, NZ):
        zd = (z + step) % NZ
        remote(gains.at[z], gains.at[z], gain_s, gain_r.at[z], zd, f).start()
    send_quad(quads[3], skip=(z + NZ // 2) % NZ)
    pass_stop(mid_back, stop_back, zb_s, stop_r.at[1], zb_r)

    def back_xy(qd, start=0, count=4):
        for t in range(count):
            zs = qd * 4 + start + t
            await_bytes(mid_back.at[zs], zb_r.at[zs])

            @pl.when(zs != z)
            def _():
                await_bytes(gains.at[zs], gain_r.at[zs])

            mid_back[zs] = (mid_back[zs].astype(F32) * gains[zs].reshape(1, 1, LANES)).astype(BF16)
        for i in range(NQ):
            d = (f % NQ + i) % NQ
            fd = m * NQ + d
            src = mid_back.at[pl.ds(qd * 4 + start, count), d]
            dst = final.at[own_q, pl.ds(qd * 4 + start, count)]
            if i > 0:
                remote(src, dst, xb_s.at[qd], xb_r.at[qd], z, fd).start()
                continue

            @pl.when(x != m)
            def _():
                remote(src, dst, xb_s.at[qd], xb_r.at[qd], z, fd).start()

            @pl.when(x == m)
            def _():
                local(src, dst, xb_r.at[qd]).start()

    def gram_left():
        rows = pl.ds(pl.multiple_of(m * QUARTER, QUARTER), QUARTER)
        for j in range(GROUP):
            gram = jnp.zeros((QUARTER, QUARTER), F32)
            for c in range(4):
                gram += lax.dot_general(
                    block[c, rows, :], block[c, j * QUARTER : (j + 1) * QUARTER, :], NT, preferred_element_type=F32
                )
            cols = slice(j * QUARTER, (j + 1) * QUARTER)
            lnew[:, cols] = (BETA * lfac[:, cols].astype(F32) + (1.0 - BETA) / B * gram).astype(BF16)

    def gram_right():
        for j in range(GROUP):
            gram = lax.dot_general(block[m], block[j], TN, preferred_element_type=F32)
            cols = slice(j * QUARTER, (j + 1) * QUARTER)
            rnew[:, cols] = (BETA * rfac[:, cols].astype(F32) + (1.0 - BETA) / B * gram).astype(BF16)

    loads[3].wait()
    gram_left()
    stores = [local(lnew, ln_out, out_sem.at[0]), local(rnew, rn_out, out_sem.at[1])]
    stores[0].start()
    back_xy(quads[0])
    loads[4].wait()
    gram_right()
    stores[1].start()
    back_xy(quads[1])
    back_xy(quads[2])
    back_xy(quads[3], early, 2)
    back_xy(quads[3], 2 - early, 2)

    for qd in quads:
        await_bytes(final.at[:, pl.ds(qd * 4, 4)], xb_r.at[qd])

    await_bytes(send_fwd, zf_s)
    await_bytes(send_back, zb_s)
    for c in range(4):
        await_bytes(raw.at[pl.ds(0, 15), 0, pl.ds(0, 4)], xf_s.at[c])
        await_bytes(raw.at[:, 0, pl.ds(0, 4)], sib_s.at[c])

        @pl.when(x == m)
        def _():
            await_bytes(final.at[pl.ds(0, NQ - 1), pl.ds(0, 4)], xb_s.at[c])

        @pl.when(x != m)
        def _():
            await_bytes(final.at[:, pl.ds(0, 4)], xb_s.at[c])

    await_bytes(gains.at[pl.ds(0, NZ - 1)], gain_s)
    for i in range(3):
        await_bytes(rroot.at[0], r_s.at[i])
        await_bytes(sums.at[0], ex_s.at[i])
    stores[0].wait()
    stores[1].wait()


def finish(owner_ref, final, lnew, rnew, dir_out, ln_out, rn_out, rows_in, wide, dirv, lvmem, rvmem, in_sem, out_sem):
    loads = [pltpu.make_async_copy(final.at[q], rows_in.at[q], in_sem.at[q]) for q in range(NQ)]
    stores = [
        pltpu.make_async_copy(lvmem, ln_out, out_sem.at[0]),
        pltpu.make_async_copy(rvmem, rn_out, out_sem.at[1]),
    ]
    for i, at in enumerate((0, 1024, 512, 1536)):
        rows = pl.ds(at, 512)
        stores.append(pltpu.make_async_copy(dirv.at[rows], dir_out.at[rows], out_sem.at[2 + i]))
    loads.append(pltpu.make_async_copy(lnew, lvmem, in_sem.at[NQ]))
    loads.append(pltpu.make_async_copy(rnew, rvmem, in_sem.at[NQ + 1]))
    for copy in loads:
        copy.start()
    row = lax.broadcasted_iota(jnp.int32, (LANES, LANES), 0)
    slot_of = (row % NZ) * NQ + row // NZ
    place = (jnp.broadcast_to(owner_ref[...], (LANES, LANES)) == slot_of).astype(BF16)
    for q in range(NQ):
        loads[q].wait()
        wide[q * 256 : q * 256 + 256, :] = rows_in[q].reshape(256, LANES).astype(F32)
    for i in range(2):
        loads[NQ + i].wait()
        stores[i].start()
    for t in range(16):
        rows = wide[pl.ds(t, LANES, stride=16), :].astype(BF16)
        blocks = lax.dot_general(rows, place, TN, preferred_element_type=F32).astype(BF16)
        dirv[t * 64 : t * 64 + 64, :] = blocks[:64]
        dirv[(16 + t) * 64 : (16 + t) * 64 + 64, :] = blocks[64:]
        if t == 7:
            stores[2].start()
            stores[3].start()
    stores[4].start()
    stores[5].start()
    for copy in stores:
        copy.wait()


def per_device(gradient, owner_slot, left_factor, right_factor, left_root, right_root):
    blocks, row_width, col_width = gradient.shape
    columns = gradient.transpose(1, 2, 0).reshape(row_width * col_width, blocks)
    anywhere = pl.BlockSpec(memory_space=pl.ANY)
    factor = jax.ShapeDtypeStruct((QUARTER, B), BF16)
    dma = pltpu.SemaphoreType.DMA
    owner = owner_slot.reshape(1, blocks)
    final, left_new, right_new = pl.pallas_call(
        kernel,
        out_shape=(jax.ShapeDtypeStruct((NQ, NZ, 16, LANES), BF16), factor, factor),
        in_specs=[pl.BlockSpec(memory_space=pltpu.VMEM)] + [anywhere] * 5,
        out_specs=(anywhere, anywhere, anywhere),
        scratch_shapes=[
            pltpu.VMEM((2048, LANES), BF16),
            pltpu.VMEM((2048, LANES), F32),
            pltpu.VMEM((NZ, NQ, 16, LANES), BF16),
            pltpu.VMEM((NZ, NQ, 16, LANES), BF16),
            pltpu.VMEM((NF // 2, 2, NZ, 16, LANES), BF16),
            pltpu.VMEM((4, B, QUARTER), BF16),
            pltpu.VMEM((QUARTER, B), BF16),
            pltpu.VMEM((GROUP, QUARTER, B), BF16),
            pltpu.VMEM((QUARTER, B), BF16),
            pltpu.VMEM((QUARTER, B), BF16),
            pltpu.VMEM((4, QUARTER, QUARTER), BF16),
            pltpu.VMEM((GROUP, QUARTER, QUARTER), F32),
            pltpu.VMEM((NZ, 1, LANES), F32),
            pltpu.VMEM((GROUP, 2, 8, LANES), F32),
            pltpu.VMEM((NZ, NQ, 16, LANES), BF16),
            pltpu.VMEM((NZ, NQ, 16, LANES), BF16),
            pltpu.VMEM((QUARTER, B), BF16),
            pltpu.VMEM((QUARTER, B), BF16),
            pltpu.VMEM((NQ, 16, LANES), BF16),
            pltpu.VMEM((NQ, 16, LANES), BF16),
            dma((5,)), dma((2,)),
            dma, dma((NZ,)),
            dma((4,)), dma((4, 4)),
            dma((4,)), dma((4,)),
            dma((3,)), dma((3,)),
            dma((3,)), dma((GROUP,)),
            dma, dma((NZ,)),
            dma, dma((NZ,)),
            dma((4,)), dma((4,)),
            dma((2,)),
        ],
        compiler_params=pltpu.CompilerParams(
            collective_id=0, has_side_effects=True, vmem_limit_bytes=60 * 1024 * 1024
        ),
        cost_estimate=pl.CostEstimate(flops=2_200_000_000, bytes_accessed=8_000_000, transcendentals=0),
    )(owner, columns, left_factor, right_factor, left_root, right_root)
    direction, left_new, right_new = pl.pallas_call(
        finish,
        out_shape=(jax.ShapeDtypeStruct(columns.shape, BF16), factor, factor),
        in_specs=[pl.BlockSpec(memory_space=pltpu.VMEM)] + [anywhere] * 3,
        out_specs=(anywhere, anywhere, anywhere),
        scratch_shapes=[
            pltpu.VMEM((NQ, NZ, 16, LANES), BF16),
            pltpu.VMEM((2048, LANES), F32),
            pltpu.VMEM((2048, LANES), BF16),
            pltpu.VMEM((QUARTER, B), BF16),
            pltpu.VMEM((QUARTER, B), BF16),
            dma((NQ + 2,)),
            dma((6,)),
        ],
        compiler_params=pltpu.CompilerParams(vmem_limit_bytes=60 * 1024 * 1024),
        cost_estimate=pl.CostEstimate(flops=70_000_000, bytes_accessed=4_000_000, transcendentals=0),
    )(owner, final, left_new, right_new)
    return direction.reshape(row_width, col_width, blocks).transpose(2, 0, 1), left_new, right_new


def solution(mesh):
    placed = (
        P(None, "fsdp", "rep"),
        P(),
        P(("rep", "fsdp"), None),
        P(("rep", "fsdp"), None),
        P(("rep", "fsdp"), None),
        P(("rep", "fsdp"), None),
    )
    return jax.shard_map(
        per_device,
        mesh=mesh,
        in_specs=placed,
        out_specs=(P(None, "fsdp", "rep"), P(("rep", "fsdp"), None), P(("rep", "fsdp"), None)),
        check_vma=False,
    )
```

```python
import functools

import jax
import jax.numpy as jnp
from jax import lax
from jax.experimental import pallas as pl
from jax.experimental.pallas import tpu as pltpu
from jax.sharding import PartitionSpec as P

MESH = pl.DeviceIdType.MESH
F32 = jnp.float32
BF16 = jnp.bfloat16
B = 1024
GROUP = 4
BETA = 0.9
EPS = 1e-06
NZ = 16
NF = 32
NQ = NF // GROUP
QUARTER = B // GROUP
LANES = 128
NT = (((1,), (1,)), ((), ()))
TN = (((0,), (0,)), ((), ()))
def in_turn(count):
    return [0] + [sign * i for i in range(1, count // 2) for sign in (1, -1)] + [count // 2]


def halves(even, odd):
    lane = lax.broadcasted_iota(jnp.int32, even.shape, even.ndim - 1)
    low = lane < LANES // 2
    axis = even.ndim - 1
    top = jnp.where(low, even, pltpu.roll(odd, LANES // 2, axis))
    bottom = jnp.where(low, pltpu.roll(even, LANES // 2, axis), odd)
    return top, bottom


def kernel(
    owner_ref, grad_in, lf_in, rf_in, lr_in, rr_in,
    final, ln_out, rn_out,
    grad, wide, send_fwd, mid_fwd, raw, block, lroot, rroot, lfac, rfac,
    tpart, acc, gains, sums, send_back, mid_back, lnew, rnew, stop_fwd, stop_back,
    in_sem, out_sem, zf_s, zf_r, xf_s, xf_r, sib_s, sib_r, r_s, r_r,
    ex_s, ex_r, gain_s, gain_r, zb_s, zb_r, xb_s, xb_r, stop_r,
):
    z = lax.axis_index("rep")
    f = lax.axis_index("fsdp")
    core = f % 2
    xy = f // 2
    m = f % GROUP
    own_q = f // GROUP
    x = f // 8
    zq = z // 4
    sibling = f + 1 - 2 * core
    across = f + 2 - 4 * (m // 2)
    m_across = m + 2 - 4 * (m // 2)
    near = 1 + 2 * (1 - (z % 4) // 2)
    quads = [zq, (zq + near) % 4, (zq + 4 - near) % 4, (zq + 2) % 4]

    def local(src, dst, sem):
        return pltpu.make_async_copy(src, dst, sem)

    def remote(src, dst, send, recv, zd, fd):
        return pltpu.make_async_remote_copy(
            src_ref=src, dst_ref=dst, send_sem=send, recv_sem=recv,
            device_id=(zd, fd), device_id_type=MESH,
        )

    def await_bytes(ref, sem):
        pltpu.make_async_copy(ref, ref, sem).wait()

    loads = [
        local(grad_in, grad, in_sem.at[0]),
        local(lr_in, lroot, in_sem.at[1]),
        local(rr_in, rroot.at[m], in_sem.at[2]),
        local(lf_in, lfac, in_sem.at[3]),
        local(rf_in, rfac, in_sem.at[4]),
    ]
    for load in loads:
        load.start()
    barrier = pltpu.get_barrier_semaphore()

    def greet_plane(i, carry):
        pl.semaphore_signal(barrier, inc=1, device_id=(z, (f + i) % NF), device_id_type=MESH)
        return carry

    def greet_ring(i, carry):
        pl.semaphore_signal(barrier, inc=1, device_id=((z + i) % NZ, f), device_id_type=MESH)
        return carry

    lax.fori_loop(1, NZ, greet_ring, 0)
    lax.fori_loop(1, NF, greet_plane, 0)

    owner = owner_ref[...]
    slot_row = lax.broadcasted_iota(jnp.int32, (LANES, LANES), 0)
    pick = (jnp.broadcast_to(owner, (LANES, LANES)) == slot_row).astype(BF16)
    loads[0].wait()
    for t in range(16):
        piece = jnp.concatenate((grad[t * 64 : t * 64 + 64, :], grad[(16 + t) * 64 : (16 + t) * 64 + 64, :]), axis=0)
        wide[pl.ds(t, LANES, stride=16), :] = lax.dot_general(pick, piece, NT, preferred_element_type=F32)
    for zd in range(NZ):
        send_fwd[zd] = wide[zd * 128 : zd * 128 + 128, :].reshape(NQ, 16, LANES).astype(BF16)

    pl.semaphore_wait(barrier, NZ - 1 + NF - 1)

    way = 1 - 2 * core

    def send_z(send, mid, send_sem, recv_sem, step):
        zd = (z + step * way + NZ) % NZ
        remote(send.at[zd], mid.at[z], send_sem, recv_sem.at[z], zd, f).start()

    def send_stop(send, stop, send_sem, recv_sem):
        zd = (z + way + NZ) % NZ
        remote(send.at[(z + NZ // 2) % NZ], stop, send_sem, recv_sem, zd, f).start()

    def pass_stop(mid, stop, send_sem, stop_sem, recv_sem):
        await_bytes(stop, stop_sem)
        origin = (z - way + NZ) % NZ
        zd = (z + 7 * way + NZ) % NZ
        remote(stop, mid.at[origin], send_sem, recv_sem.at[origin], zd, f).start()

    def send_root(member, index, fd, parts):
        for part in parts:
            rows = rroot.at[member, pl.ds(part * 64, 64)]
            remote(rows, rows, r_s.at[index], r_r.at[index], z, fd).start()

    loads[2].wait()
    send_stop(send_fwd, stop_fwd, zf_s, stop_r.at[0])
    for step in range(1, 6):
        for sign in (1, -1):
            send_z(send_fwd, mid_fwd, zf_s, zf_r, sign * step)
        if step < 5:
            send_root(m, 0, across, (step - 1,))
    local(send_fwd.at[z], mid_fwd.at[z], zf_r.at[z]).start()
    send_root(m, 1, sibling, range(4))
    pass_stop(mid_fwd, stop_fwd, zf_s, stop_r.at[0], zf_r)

    def forward_xy(qd):
        for t in range(4):
            await_bytes(mid_fwd.at[qd * 4 + t], zf_r.at[qd * 4 + t])

        for i in in_turn(NF // 2):
            chip = (xy + i * way + NF // 2) % (NF // 2)
            q = chip // 2
            src = mid_fwd.at[pl.ds(qd * 4, 4), q]
            dst = raw.at[xy, core, pl.ds(qd * 4, 4)]
            if i == 0:
                local(src, dst, xf_r.at[qd, x]).start()
            else:
                remote(src, dst, xf_s.at[qd], xf_r.at[qd, x], z, chip * 2 + core).start()

    def share(qd):
        for i in range(4):
            column = (x + i) % 4
            mine = raw.at[pl.ds(column * 4, 4), core, pl.ds(qd * 4, 4)]
            await_bytes(mine, xf_r.at[qd, column])
            remote(mine, mine, sib_s.at[qd], sib_r.at[qd], z, sibling).start()

    def gather_chunk(qd):
        await_bytes(raw.at[:, 1 - core, pl.ds(qd * 4, 4)], sib_r.at[qd])

        def unpack(i, carry):
            for pair in range(2):
                first = qd * 4 + 2 * pair
                even = raw[pl.ds(i * 2, 2), :, first].reshape(64, LANES)
                odd = raw[pl.ds(i * 2, 2), :, first + 1].reshape(64, LANES)
                top, bottom = halves(even, odd)
                rows = jnp.concatenate((top.reshape(4, 16, LANES), bottom.reshape(4, 16, LANES)), axis=1)
                at = pl.multiple_of(i * 128, 128)
                block[qd, pl.ds(at, 128), pair * LANES : (pair + 1) * LANES] = rows.reshape(128, LANES)
            return carry

        lax.fori_loop(0, NF // 4, unpack, 0)

    def left_product(qd):
        tpart[qd] = jnp.dot(lroot[...], block[qd], preferred_element_type=F32).astype(BF16)

    def right_part(qd, j):
        return lax.dot_general(
            tpart[qd], rroot[j, :, pl.ds(pl.multiple_of(qd * QUARTER, QUARTER), QUARTER)], NT,
            preferred_element_type=F32,
        )

    def right_product(qd, first=False):
        for j in range(GROUP):
            if first:
                acc[j] = right_part(qd, j)
            else:
                acc[j] += right_part(qd, j)

    def grad_squares(qd, total):
        rows = block[qd, pl.ds(pl.multiple_of(m * QUARTER, QUARTER), QUARTER), :].astype(F32)
        return total + jnp.sum((rows * rows).reshape(QUARTER // 8, 8, 2, LANES), axis=(0, 2))

    total = jnp.zeros((8, LANES), F32)
    forward_xy(quads[0])
    for step in (6, 7):
        for sign in (1, -1):
            send_z(send_fwd, mid_fwd, zf_s, zf_r, sign * step)
    forward_xy(quads[1])
    loads[1].wait()
    share(quads[0])
    forward_xy(quads[2])
    share(quads[1])
    gather_chunk(quads[0])
    left_product(quads[0])
    total = grad_squares(quads[0], total)
    await_bytes(rroot.at[m_across], r_r.at[0])
    send_root(m_across, 2, sibling, range(4))
    forward_xy(quads[3])
    share(quads[2])
    gather_chunk(quads[1])
    left_product(quads[1])
    total = grad_squares(quads[1], total)
    await_bytes(rroot.at[0], r_r.at[1])
    await_bytes(rroot.at[0], r_r.at[2])
    right_product(quads[0], first=True)
    right_product(quads[1])
    share(quads[3])
    gather_chunk(quads[2])
    left_product(quads[2])
    total = grad_squares(quads[2], total)
    right_product(quads[2])
    gather_chunk(quads[3])
    left_product(quads[3])

    prec_total = jnp.zeros((8, LANES), F32)
    for c in range(4):
        value = (acc[c] + right_part(quads[3], c)).astype(BF16)
        for pair in range(2):
            rows = value[:, pair * LANES : (pair + 1) * LANES].reshape(NQ, 2, 16, LANES)
            even, odd = halves(rows[:, 0].reshape(LANES, LANES), rows[:, 1].reshape(LANES, LANES))
            send_back[c * 4 + 2 * pair] = even.reshape(NQ, 16, LANES)
            send_back[c * 4 + 2 * pair + 1] = odd.reshape(NQ, 16, LANES)
        wider = value.astype(F32)
        prec_total += jnp.sum((wider * wider).reshape(QUARTER // 8, 8, 2, LANES), axis=(0, 2))

    sums[m, 0] = grad_squares(quads[3], total)
    sums[m, 1] = prec_total
    for step in range(1, GROUP):
        fd = own_q * GROUP + (m + step) % GROUP
        remote(sums.at[m], sums.at[m], ex_s.at[step - 1], ex_r.at[m], z, fd).start()
    send_stop(send_back, stop_back, zb_s, stop_r.at[1])
    for step in (1, 2, 3):
        for sign in (1, -1):
            send_z(send_back, mid_back, zb_s, zb_r, sign * step)
    local(send_back.at[z], mid_back.at[z], zb_r.at[z]).start()
    for step in range(1, GROUP):
        await_bytes(sums.at[0], ex_r.at[(m + step) % GROUP])
    grad_sq = jnp.sum(sums[0, 0] + sums[1, 0] + sums[2, 0] + sums[3, 0], keepdims=True)
    prec_sq = jnp.sum(sums[0, 1] + sums[1, 1] + sums[2, 1] + sums[3, 1], keepdims=True)
    gains[z] = jnp.broadcast_to(jnp.sqrt((grad_sq + EPS) / (prec_sq + EPS)), (1, LANES))
    for step in range(1, NZ):
        zd = (z + step) % NZ
        remote(gains.at[z], gains.at[z], gain_s, gain_r.at[z], zd, f).start()
    for step in (4, 5, 6, 7):
        for sign in (1, -1):
            send_z(send_back, mid_back, zb_s, zb_r, sign * step)
    pass_stop(mid_back, stop_back, zb_s, stop_r.at[1], zb_r)

    def back_xy(qd):
        for t in range(4):
            zs = qd * 4 + t
            await_bytes(mid_back.at[zs], zb_r.at[zs])

            @pl.when(zs != z)
            def _():
                await_bytes(gains.at[zs], gain_r.at[zs])

            mid_back[zs] = (mid_back[zs].astype(F32) * gains[zs].reshape(1, 1, LANES)).astype(BF16)
        for i in in_turn(NQ):
            d = (f % NQ + i * way + NQ) % NQ
            fd = m * NQ + d
            src = mid_back.at[pl.ds(qd * 4, 4), d]
            dst = final.at[own_q, pl.ds(qd * 4, 4)]
            if i != 0:
                remote(src, dst, xb_s.at[qd], xb_r.at[qd], z, fd).start()
                continue

            @pl.when(x != m)
            def _():
                remote(src, dst, xb_s.at[qd], xb_r.at[qd], z, fd).start()

            @pl.when(x == m)
            def _():
                local(src, dst, xb_r.at[qd]).start()

    def gram_left():
        rows = pl.ds(pl.multiple_of(m * QUARTER, QUARTER), QUARTER)
        for j in range(GROUP):
            gram = jnp.zeros((QUARTER, QUARTER), F32)
            for c in range(4):
                gram += lax.dot_general(
                    block[c, rows, :], block[c, j * QUARTER : (j + 1) * QUARTER, :], NT, preferred_element_type=F32
                )
            cols = slice(j * QUARTER, (j + 1) * QUARTER)
            lnew[:, cols] = (BETA * lfac[:, cols].astype(F32) + (1.0 - BETA) / B * gram).astype(BF16)

    def gram_right():
        for j in range(GROUP):
            gram = lax.dot_general(block[m], block[j], TN, preferred_element_type=F32)
            cols = slice(j * QUARTER, (j + 1) * QUARTER)
            rnew[:, cols] = (BETA * rfac[:, cols].astype(F32) + (1.0 - BETA) / B * gram).astype(BF16)

    loads[3].wait()
    gram_left()
    stores = [local(lnew, ln_out, out_sem.at[0]), local(rnew, rn_out, out_sem.at[1])]
    stores[0].start()
    back_xy(quads[0])
    loads[4].wait()
    gram_right()
    stores[1].start()
    back_xy(quads[1])
    back_xy(quads[2])
    back_xy(quads[3])

    for qd in quads:
        await_bytes(final.at[:, pl.ds(qd * 4, 4)], xb_r.at[qd])

    await_bytes(send_fwd, zf_s)
    await_bytes(send_back, zb_s)
    for c in range(4):
        await_bytes(raw.at[pl.ds(0, 15), 0, pl.ds(0, 4)], xf_s.at[c])
        await_bytes(raw.at[:, 0, pl.ds(0, 4)], sib_s.at[c])

        @pl.when(x == m)
        def _():
            await_bytes(final.at[pl.ds(0, NQ - 1), pl.ds(0, 4)], xb_s.at[c])

        @pl.when(x != m)
        def _():
            await_bytes(final.at[:, pl.ds(0, 4)], xb_s.at[c])

    await_bytes(gains.at[pl.ds(0, NZ - 1)], gain_s)
    for i in range(3):
        await_bytes(rroot.at[0], r_s.at[i])
        await_bytes(sums.at[0], ex_s.at[i])
    stores[0].wait()
    stores[1].wait()


def finish(owner_ref, final, lnew, rnew, dir_out, ln_out, rn_out, rows_in, wide, dirv, lvmem, rvmem, in_sem, out_sem):
    loads = [pltpu.make_async_copy(final.at[q], rows_in.at[q], in_sem.at[q]) for q in range(NQ)]
    stores = [
        pltpu.make_async_copy(lvmem, ln_out, out_sem.at[0]),
        pltpu.make_async_copy(rvmem, rn_out, out_sem.at[1]),
    ]
    for i, at in enumerate((0, 1024, 512, 1536)):
        rows = pl.ds(at, 512)
        stores.append(pltpu.make_async_copy(dirv.at[rows], dir_out.at[rows], out_sem.at[2 + i]))
    loads.append(pltpu.make_async_copy(lnew, lvmem, in_sem.at[NQ]))
    loads.append(pltpu.make_async_copy(rnew, rvmem, in_sem.at[NQ + 1]))
    for copy in loads:
        copy.start()
    row = lax.broadcasted_iota(jnp.int32, (LANES, LANES), 0)
    slot_of = (row % NZ) * NQ + row // NZ
    place = (jnp.broadcast_to(owner_ref[...], (LANES, LANES)) == slot_of).astype(BF16)
    for q in range(NQ):
        loads[q].wait()
        wide[q * 256 : q * 256 + 256, :] = rows_in[q].reshape(256, LANES).astype(F32)
    for i in range(2):
        loads[NQ + i].wait()
        stores[i].start()
    for t in range(16):
        rows = wide[pl.ds(t, LANES, stride=16), :].astype(BF16)
        blocks = lax.dot_general(rows, place, TN, preferred_element_type=F32).astype(BF16)
        dirv[t * 64 : t * 64 + 64, :] = blocks[:64]
        dirv[(16 + t) * 64 : (16 + t) * 64 + 64, :] = blocks[64:]
        if t == 7:
            stores[2].start()
            stores[3].start()
    stores[4].start()
    stores[5].start()
    for copy in stores:
        copy.wait()


def per_device(gradient, owner_slot, left_factor, right_factor, left_root, right_root):
    blocks, row_width, col_width = gradient.shape
    columns = gradient.transpose(1, 2, 0).reshape(row_width * col_width, blocks)
    anywhere = pl.BlockSpec(memory_space=pl.ANY)
    factor = jax.ShapeDtypeStruct((QUARTER, B), BF16)
    dma = pltpu.SemaphoreType.DMA
    owner = owner_slot.reshape(1, blocks)
    final, left_new, right_new = pl.pallas_call(
        kernel,
        out_shape=(jax.ShapeDtypeStruct((NQ, NZ, 16, LANES), BF16), factor, factor),
        in_specs=[pl.BlockSpec(memory_space=pltpu.VMEM)] + [anywhere] * 5,
        out_specs=(anywhere, anywhere, anywhere),
        scratch_shapes=[
            pltpu.VMEM((2048, LANES), BF16),
            pltpu.VMEM((2048, LANES), F32),
            pltpu.VMEM((NZ, NQ, 16, LANES), BF16),
            pltpu.VMEM((NZ, NQ, 16, LANES), BF16),
            pltpu.VMEM((NF // 2, 2, NZ, 16, LANES), BF16),
            pltpu.VMEM((4, B, QUARTER), BF16),
            pltpu.VMEM((QUARTER, B), BF16),
            pltpu.VMEM((GROUP, QUARTER, B), BF16),
            pltpu.VMEM((QUARTER, B), BF16),
            pltpu.VMEM((QUARTER, B), BF16),
            pltpu.VMEM((4, QUARTER, QUARTER), BF16),
            pltpu.VMEM((GROUP, QUARTER, QUARTER), F32),
            pltpu.VMEM((NZ, 1, LANES), F32),
            pltpu.VMEM((GROUP, 2, 8, LANES), F32),
            pltpu.VMEM((NZ, NQ, 16, LANES), BF16),
            pltpu.VMEM((NZ, NQ, 16, LANES), BF16),
            pltpu.VMEM((QUARTER, B), BF16),
            pltpu.VMEM((QUARTER, B), BF16),
            pltpu.VMEM((NQ, 16, LANES), BF16),
            pltpu.VMEM((NQ, 16, LANES), BF16),
            dma((5,)), dma((2,)),
            dma, dma((NZ,)),
            dma((4,)), dma((4, 4)),
            dma((4,)), dma((4,)),
            dma((3,)), dma((3,)),
            dma((3,)), dma((GROUP,)),
            dma, dma((NZ,)),
            dma, dma((NZ,)),
            dma((4,)), dma((4,)),
            dma((2,)),
        ],
        compiler_params=pltpu.CompilerParams(
            collective_id=0, has_side_effects=True, vmem_limit_bytes=60 * 1024 * 1024
        ),
        cost_estimate=pl.CostEstimate(flops=2_200_000_000, bytes_accessed=8_000_000, transcendentals=0),
    )(owner, columns, left_factor, right_factor, left_root, right_root)
    direction, left_new, right_new = pl.pallas_call(
        finish,
        out_shape=(jax.ShapeDtypeStruct(columns.shape, BF16), factor, factor),
        in_specs=[pl.BlockSpec(memory_space=pltpu.VMEM)] + [anywhere] * 3,
        out_specs=(anywhere, anywhere, anywhere),
        scratch_shapes=[
            pltpu.VMEM((NQ, NZ, 16, LANES), BF16),
            pltpu.VMEM((2048, LANES), F32),
            pltpu.VMEM((2048, LANES), BF16),
            pltpu.VMEM((QUARTER, B), BF16),
            pltpu.VMEM((QUARTER, B), BF16),
            dma((NQ + 2,)),
            dma((6,)),
        ],
        compiler_params=pltpu.CompilerParams(vmem_limit_bytes=60 * 1024 * 1024),
        cost_estimate=pl.CostEstimate(flops=70_000_000, bytes_accessed=4_000_000, transcendentals=0),
    )(owner, final, left_new, right_new)
    return direction.reshape(row_width, col_width, blocks).transpose(2, 0, 1), left_new, right_new


def solution(mesh):
    placed = (
        P(None, "fsdp", "rep"),
        P(),
        P(("rep", "fsdp"), None),
        P(("rep", "fsdp"), None),
        P(("rep", "fsdp"), None),
        P(("rep", "fsdp"), None),
    )
    return jax.shard_map(
        per_device,
        mesh=mesh,
        in_specs=placed,
        out_specs=(P(None, "fsdp", "rep"), P(("rep", "fsdp"), None), P(("rep", "fsdp"), None)),
        check_vma=False,
    )
```

```python
import functools

import jax
import jax.numpy as jnp
from jax import lax
from jax.experimental import pallas as pl
from jax.experimental.pallas import tpu as pltpu
from jax.sharding import PartitionSpec as P

MESH = pl.DeviceIdType.MESH
F32 = jnp.float32
BF16 = jnp.bfloat16
B = 1024
GROUP = 4
BETA = 0.9
EPS = 1e-06
NZ = 16
NF = 32
NQ = NF // GROUP
QUARTER = B // GROUP
LANES = 128
NT = (((1,), (1,)), ((), ()))
TN = (((0,), (0,)), ((), ()))
def in_turn(count):
    return [0] + [sign * i for i in range(1, count // 2) for sign in (1, -1)] + [count // 2]


def halves(even, odd):
    lane = lax.broadcasted_iota(jnp.int32, even.shape, even.ndim - 1)
    low = lane < LANES // 2
    axis = even.ndim - 1
    top = jnp.where(low, even, pltpu.roll(odd, LANES // 2, axis))
    bottom = jnp.where(low, pltpu.roll(even, LANES // 2, axis), odd)
    return top, bottom


def kernel(
    owner_ref, grad_in, lf_in, rf_in, lr_in, rr_in,
    final, ln_out, rn_out,
    grad, wide, send_fwd, mid_fwd, raw, block, lroot, rroot, lfac, rfac,
    tpart, acc, gains, sums, send_back, mid_back, lnew, rnew, stop_fwd, stop_back,
    in_sem, out_sem, zf_s, zf_r, xf_s, xf_r, sib_s, sib_r, r_s, r_r,
    ex_s, ex_r, gain_s, gain_r, zb_s, zb_r, xb_s, xb_r, stop_r,
):
    z = lax.axis_index("rep")
    f = lax.axis_index("fsdp")
    core = f % 2
    xy = f // 2
    m = f % GROUP
    own_q = f // GROUP
    x = f // 8
    zq = z // 4
    sibling = f + 1 - 2 * core
    across = f + 2 - 4 * (m // 2)
    m_across = m + 2 - 4 * (m // 2)
    near = 1 + 2 * (1 - (z % 4) // 2)
    quads = [zq, (zq + near) % 4, (zq + 4 - near) % 4, (zq + 2) % 4]

    def local(src, dst, sem):
        return pltpu.make_async_copy(src, dst, sem)

    def remote(src, dst, send, recv, zd, fd):
        return pltpu.make_async_remote_copy(
            src_ref=src, dst_ref=dst, send_sem=send, recv_sem=recv,
            device_id=(zd, fd), device_id_type=MESH,
        )

    def await_bytes(ref, sem):
        pltpu.make_async_copy(ref, ref, sem).wait()

    loads = [
        local(grad_in, grad, in_sem.at[0]),
        local(lr_in, lroot, in_sem.at[1]),
        local(rr_in, rroot.at[m], in_sem.at[2]),
        local(lf_in, lfac, in_sem.at[3]),
        local(rf_in, rfac, in_sem.at[4]),
    ]
    for load in loads:
        load.start()
    barrier = pltpu.get_barrier_semaphore()

    def greet(fd):
        pl.semaphore_signal(barrier, inc=1, device_id=(z, fd), device_id_type=MESH)

    def greet_plane(i, carry):
        greet((xy + i) % (NF // 2) * 2 + core)
        return carry

    def greet_back(i, carry):
        greet(i * GROUP + x)
        return carry

    def greet_ring(i, carry):
        pl.semaphore_signal(barrier, inc=1, device_id=((z + i) % NZ, f), device_id_type=MESH)
        return carry

    lax.fori_loop(1, NZ, greet_ring, 0)
    lax.fori_loop(1, NF // 2, greet_plane, 0)
    greet(sibling)
    greet(across + 1 - 2 * core)

    @pl.when(x % 2 != core)
    def _():
        lax.fori_loop(0, NQ, greet_back, 0)

    owner = owner_ref[...]
    slot_row = lax.broadcasted_iota(jnp.int32, (LANES, LANES), 0)
    pick = (jnp.broadcast_to(owner, (LANES, LANES)) == slot_row).astype(BF16)
    loads[0].wait()
    for t in range(16):
        piece = jnp.concatenate((grad[t * 64 : t * 64 + 64, :], grad[(16 + t) * 64 : (16 + t) * 64 + 64, :]), axis=0)
        wide[pl.ds(t, LANES, stride=16), :] = lax.dot_general(pick, piece, NT, preferred_element_type=F32)
    for zd in range(NZ):
        send_fwd[zd] = wide[zd * 128 : zd * 128 + 128, :].reshape(NQ, 16, LANES).astype(BF16)

    pl.semaphore_wait(barrier, NZ - 1 + NF // 2 - 1 + 2 + 4)

    way = 1 - 2 * core

    def send_z(send, mid, send_sem, recv_sem, step):
        zd = (z + step * way + NZ) % NZ
        remote(send.at[zd], mid.at[z], send_sem, recv_sem.at[z], zd, f).start()

    def send_stop(send, stop, send_sem, recv_sem):
        zd = (z + way + NZ) % NZ
        remote(send.at[(z + NZ // 2) % NZ], stop, send_sem, recv_sem, zd, f).start()

    def pass_stop(mid, stop, send_sem, stop_sem, recv_sem):
        await_bytes(stop, stop_sem)
        origin = (z - way + NZ) % NZ
        zd = (z + 7 * way + NZ) % NZ
        remote(stop, mid.at[origin], send_sem, recv_sem.at[origin], zd, f).start()

    def send_root(member, index, fd, parts):
        for part in parts:
            rows = rroot.at[member, pl.ds(part * 64, 64)]
            remote(rows, rows, r_s.at[index], r_r.at[index], z, fd).start()

    loads[2].wait()
    send_stop(send_fwd, stop_fwd, zf_s, stop_r.at[0])
    for step in range(1, 6):
        for sign in (1, -1):
            send_z(send_fwd, mid_fwd, zf_s, zf_r, sign * step)
        if step < 5:
            send_root(m, 0, across, (step - 1,))
    local(send_fwd.at[z], mid_fwd.at[z], zf_r.at[z]).start()
    send_root(m, 1, sibling, range(4))
    pass_stop(mid_fwd, stop_fwd, zf_s, stop_r.at[0], zf_r)

    def forward_xy(qd):
        for t in range(4):
            await_bytes(mid_fwd.at[qd * 4 + t], zf_r.at[qd * 4 + t])

        for i in in_turn(NF // 2):
            chip = (xy + i * way + NF // 2) % (NF // 2)
            q = chip // 2
            src = mid_fwd.at[pl.ds(qd * 4, 4), q]
            dst = raw.at[xy, core, pl.ds(qd * 4, 4)]
            if i == 0:
                local(src, dst, xf_r.at[qd, x]).start()
            else:
                remote(src, dst, xf_s.at[qd], xf_r.at[qd, x], z, chip * 2 + core).start()

    def share(qd):
        for i in range(4):
            column = (x + i) % 4
            mine = raw.at[pl.ds(column * 4, 4), core, pl.ds(qd * 4, 4)]
            await_bytes(mine, xf_r.at[qd, column])
            remote(mine, mine, sib_s.at[qd], sib_r.at[qd], z, sibling).start()

    def gather_chunk(qd):
        await_bytes(raw.at[:, 1 - core, pl.ds(qd * 4, 4)], sib_r.at[qd])

        def unpack(i, carry):
            for pair in range(2):
                first = qd * 4 + 2 * pair
                even = raw[pl.ds(i * 2, 2), :, first].reshape(64, LANES)
                odd = raw[pl.ds(i * 2, 2), :, first + 1].reshape(64, LANES)
                top, bottom = halves(even, odd)
                rows = jnp.concatenate((top.reshape(4, 16, LANES), bottom.reshape(4, 16, LANES)), axis=1)
                at = pl.multiple_of(i * 128, 128)
                block[qd, pl.ds(at, 128), pair * LANES : (pair + 1) * LANES] = rows.reshape(128, LANES)
            return carry

        lax.fori_loop(0, NF // 4, unpack, 0)

    def left_product(qd):
        tpart[qd] = jnp.dot(lroot[...], block[qd], preferred_element_type=F32).astype(BF16)

    def right_part(qd, j):
        return lax.dot_general(
            tpart[qd], rroot[j, :, pl.ds(pl.multiple_of(qd * QUARTER, QUARTER), QUARTER)], NT,
            preferred_element_type=F32,
        )

    def right_product(qd, first=False):
        for j in range(GROUP):
            if first:
                acc[j] = right_part(qd, j)
            else:
                acc[j] += right_part(qd, j)

    def grad_squares(qd, total):
        rows = block[qd, pl.ds(pl.multiple_of(m * QUARTER, QUARTER), QUARTER), :].astype(F32)
        return total + jnp.sum((rows * rows).reshape(QUARTER // 8, 8, 2, LANES), axis=(0, 2))

    total = jnp.zeros((8, LANES), F32)
    forward_xy(quads[0])
    for step in (6, 7):
        for sign in (1, -1):
            send_z(send_fwd, mid_fwd, zf_s, zf_r, sign * step)
    forward_xy(quads[1])
    loads[1].wait()
    share(quads[0])
    forward_xy(quads[2])
    share(quads[1])
    gather_chunk(quads[0])
    left_product(quads[0])
    total = grad_squares(quads[0], total)
    await_bytes(rroot.at[m_across], r_r.at[0])
    send_root(m_across, 2, sibling, range(4))
    forward_xy(quads[3])
    share(quads[2])
    gather_chunk(quads[1])
    left_product(quads[1])
    total = grad_squares(quads[1], total)
    await_bytes(rroot.at[0], r_r.at[1])
    await_bytes(rroot.at[0], r_r.at[2])
    right_product(quads[0], first=True)
    right_product(quads[1])
    share(quads[3])
    gather_chunk(quads[2])
    left_product(quads[2])
    total = grad_squares(quads[2], total)
    right_product(quads[2])
    gather_chunk(quads[3])
    left_product(quads[3])

    prec_total = jnp.zeros((8, LANES), F32)
    for c in range(4):
        value = (acc[c] + right_part(quads[3], c)).astype(BF16)
        for pair in range(2):
            rows = value[:, pair * LANES : (pair + 1) * LANES].reshape(NQ, 2, 16, LANES)
            even, odd = halves(rows[:, 0].reshape(LANES, LANES), rows[:, 1].reshape(LANES, LANES))
            send_back[c * 4 + 2 * pair] = even.reshape(NQ, 16, LANES)
            send_back[c * 4 + 2 * pair + 1] = odd.reshape(NQ, 16, LANES)
        wider = value.astype(F32)
        prec_total += jnp.sum((wider * wider).reshape(QUARTER // 8, 8, 2, LANES), axis=(0, 2))

    sums[m, 0] = grad_squares(quads[3], total)
    sums[m, 1] = prec_total
    for step in range(1, GROUP):
        fd = own_q * GROUP + (m + step) % GROUP
        remote(sums.at[m], sums.at[m], ex_s.at[step - 1], ex_r.at[m], z, fd).start()
    send_stop(send_back, stop_back, zb_s, stop_r.at[1])
    for step in (1, 2, 3):
        for sign in (1, -1):
            send_z(send_back, mid_back, zb_s, zb_r, sign * step)
    local(send_back.at[z], mid_back.at[z], zb_r.at[z]).start()
    for step in range(1, GROUP):
        await_bytes(sums.at[0], ex_r.at[(m + step) % GROUP])
    grad_sq = jnp.sum(sums[0, 0] + sums[1, 0] + sums[2, 0] + sums[3, 0], keepdims=True)
    prec_sq = jnp.sum(sums[0, 1] + sums[1, 1] + sums[2, 1] + sums[3, 1], keepdims=True)
    gains[z] = jnp.broadcast_to(jnp.sqrt((grad_sq + EPS) / (prec_sq + EPS)), (1, LANES))
    for step in range(1, NZ):
        zd = (z + step) % NZ
        remote(gains.at[z], gains.at[z], gain_s, gain_r.at[z], zd, f).start()
    for step in (4, 5, 6, 7):
        for sign in (1, -1):
            send_z(send_back, mid_back, zb_s, zb_r, sign * step)
    pass_stop(mid_back, stop_back, zb_s, stop_r.at[1], zb_r)

    def back_xy(qd):
        for t in range(4):
            zs = qd * 4 + t
            await_bytes(mid_back.at[zs], zb_r.at[zs])

            @pl.when(zs != z)
            def _():
                await_bytes(gains.at[zs], gain_r.at[zs])

            mid_back[zs] = (mid_back[zs].astype(F32) * gains[zs].reshape(1, 1, LANES)).astype(BF16)
        for i in in_turn(NQ):
            d = (f % NQ + i * way + NQ) % NQ
            fd = m * NQ + d
            src = mid_back.at[pl.ds(qd * 4, 4), d]
            dst = final.at[own_q, pl.ds(qd * 4, 4)]
            if i != 0:
                remote(src, dst, xb_s.at[qd], xb_r.at[qd], z, fd).start()
                continue

            @pl.when(x != m)
            def _():
                remote(src, dst, xb_s.at[qd], xb_r.at[qd], z, fd).start()

            @pl.when(x == m)
            def _():
                local(src, dst, xb_r.at[qd]).start()

    def gram_left():
        rows = pl.ds(pl.multiple_of(m * QUARTER, QUARTER), QUARTER)
        for j in range(GROUP):
            gram = jnp.zeros((QUARTER, QUARTER), F32)
            for c in range(4):
                gram += lax.dot_general(
                    block[c, rows, :], block[c, j * QUARTER : (j + 1) * QUARTER, :], NT, preferred_element_type=F32
                )
            cols = slice(j * QUARTER, (j + 1) * QUARTER)
            lnew[:, cols] = (BETA * lfac[:, cols].astype(F32) + (1.0 - BETA) / B * gram).astype(BF16)

    def gram_right():
        for j in range(GROUP):
            gram = lax.dot_general(block[m], block[j], TN, preferred_element_type=F32)
            cols = slice(j * QUARTER, (j + 1) * QUARTER)
            rnew[:, cols] = (BETA * rfac[:, cols].astype(F32) + (1.0 - BETA) / B * gram).astype(BF16)

    loads[3].wait()
    gram_left()
    stores = [local(lnew, ln_out, out_sem.at[0]), local(rnew, rn_out, out_sem.at[1])]
    stores[0].start()
    back_xy(quads[0])
    loads[4].wait()
    gram_right()
    stores[1].start()
    back_xy(quads[1])
    back_xy(quads[2])
    back_xy(quads[3])

    for qd in quads:
        await_bytes(final.at[:, pl.ds(qd * 4, 4)], xb_r.at[qd])

    await_bytes(send_fwd, zf_s)
    await_bytes(send_back, zb_s)
    for c in range(4):
        await_bytes(raw.at[pl.ds(0, 15), 0, pl.ds(0, 4)], xf_s.at[c])
        await_bytes(raw.at[:, 0, pl.ds(0, 4)], sib_s.at[c])

        @pl.when(x == m)
        def _():
            await_bytes(final.at[pl.ds(0, NQ - 1), pl.ds(0, 4)], xb_s.at[c])

        @pl.when(x != m)
        def _():
            await_bytes(final.at[:, pl.ds(0, 4)], xb_s.at[c])

    await_bytes(gains.at[pl.ds(0, NZ - 1)], gain_s)
    for i in range(3):
        await_bytes(rroot.at[0], r_s.at[i])
        await_bytes(sums.at[0], ex_s.at[i])
    stores[0].wait()
    stores[1].wait()


def finish(owner_ref, final, lnew, rnew, dir_out, ln_out, rn_out, rows_in, wide, dirv, lvmem, rvmem, in_sem, out_sem):
    loads = [pltpu.make_async_copy(final.at[q], rows_in.at[q], in_sem.at[q]) for q in range(NQ)]
    stores = [
        pltpu.make_async_copy(lvmem, ln_out, out_sem.at[0]),
        pltpu.make_async_copy(rvmem, rn_out, out_sem.at[1]),
    ]
    for i, at in enumerate((0, 1024, 512, 1536)):
        rows = pl.ds(at, 512)
        stores.append(pltpu.make_async_copy(dirv.at[rows], dir_out.at[rows], out_sem.at[2 + i]))
    loads.append(pltpu.make_async_copy(lnew, lvmem, in_sem.at[NQ]))
    loads.append(pltpu.make_async_copy(rnew, rvmem, in_sem.at[NQ + 1]))
    for copy in loads:
        copy.start()
    row = lax.broadcasted_iota(jnp.int32, (LANES, LANES), 0)
    slot_of = (row % NZ) * NQ + row // NZ
    place = (jnp.broadcast_to(owner_ref[...], (LANES, LANES)) == slot_of).astype(BF16)
    for q in range(NQ):
        loads[q].wait()
        wide[q * 256 : q * 256 + 256, :] = rows_in[q].reshape(256, LANES).astype(F32)
    for i in range(2):
        loads[NQ + i].wait()
        stores[i].start()
    for t in range(16):
        rows = wide[pl.ds(t, LANES, stride=16), :].astype(BF16)
        blocks = lax.dot_general(rows, place, TN, preferred_element_type=F32).astype(BF16)
        dirv[t * 64 : t * 64 + 64, :] = blocks[:64]
        dirv[(16 + t) * 64 : (16 + t) * 64 + 64, :] = blocks[64:]
        if t == 7:
            stores[2].start()
            stores[3].start()
    stores[4].start()
    stores[5].start()
    for copy in stores:
        copy.wait()


def per_device(gradient, owner_slot, left_factor, right_factor, left_root, right_root):
    blocks, row_width, col_width = gradient.shape
    columns = gradient.transpose(1, 2, 0).reshape(row_width * col_width, blocks)
    anywhere = pl.BlockSpec(memory_space=pl.ANY)
    factor = jax.ShapeDtypeStruct((QUARTER, B), BF16)
    dma = pltpu.SemaphoreType.DMA
    owner = owner_slot.reshape(1, blocks)
    final, left_new, right_new = pl.pallas_call(
        kernel,
        out_shape=(jax.ShapeDtypeStruct((NQ, NZ, 16, LANES), BF16), factor, factor),
        in_specs=[pl.BlockSpec(memory_space=pltpu.VMEM)] + [anywhere] * 5,
        out_specs=(anywhere, anywhere, anywhere),
        scratch_shapes=[
            pltpu.VMEM((2048, LANES), BF16),
            pltpu.VMEM((2048, LANES), F32),
            pltpu.VMEM((NZ, NQ, 16, LANES), BF16),
            pltpu.VMEM((NZ, NQ, 16, LANES), BF16),
            pltpu.VMEM((NF // 2, 2, NZ, 16, LANES), BF16),
            pltpu.VMEM((4, B, QUARTER), BF16),
            pltpu.VMEM((QUARTER, B), BF16),
            pltpu.VMEM((GROUP, QUARTER, B), BF16),
            pltpu.VMEM((QUARTER, B), BF16),
            pltpu.VMEM((QUARTER, B), BF16),
            pltpu.VMEM((4, QUARTER, QUARTER), BF16),
            pltpu.VMEM((GROUP, QUARTER, QUARTER), F32),
            pltpu.VMEM((NZ, 1, LANES), F32),
            pltpu.VMEM((GROUP, 2, 8, LANES), F32),
            pltpu.VMEM((NZ, NQ, 16, LANES), BF16),
            pltpu.VMEM((NZ, NQ, 16, LANES), BF16),
            pltpu.VMEM((QUARTER, B), BF16),
            pltpu.VMEM((QUARTER, B), BF16),
            pltpu.VMEM((NQ, 16, LANES), BF16),
            pltpu.VMEM((NQ, 16, LANES), BF16),
            dma((5,)), dma((2,)),
            dma, dma((NZ,)),
            dma((4,)), dma((4, 4)),
            dma((4,)), dma((4,)),
            dma((3,)), dma((3,)),
            dma((3,)), dma((GROUP,)),
            dma, dma((NZ,)),
            dma, dma((NZ,)),
            dma((4,)), dma((4,)),
            dma((2,)),
        ],
        compiler_params=pltpu.CompilerParams(
            collective_id=0, has_side_effects=True, vmem_limit_bytes=60 * 1024 * 1024
        ),
        cost_estimate=pl.CostEstimate(flops=2_200_000_000, bytes_accessed=8_000_000, transcendentals=0),
    )(owner, columns, left_factor, right_factor, left_root, right_root)
    direction, left_new, right_new = pl.pallas_call(
        finish,
        out_shape=(jax.ShapeDtypeStruct(columns.shape, BF16), factor, factor),
        in_specs=[pl.BlockSpec(memory_space=pltpu.VMEM)] + [anywhere] * 3,
        out_specs=(anywhere, anywhere, anywhere),
        scratch_shapes=[
            pltpu.VMEM((NQ, NZ, 16, LANES), BF16),
            pltpu.VMEM((2048, LANES), F32),
            pltpu.VMEM((2048, LANES), BF16),
            pltpu.VMEM((QUARTER, B), BF16),
            pltpu.VMEM((QUARTER, B), BF16),
            dma((NQ + 2,)),
            dma((6,)),
        ],
        compiler_params=pltpu.CompilerParams(vmem_limit_bytes=60 * 1024 * 1024),
        cost_estimate=pl.CostEstimate(flops=70_000_000, bytes_accessed=4_000_000, transcendentals=0),
    )(owner, final, left_new, right_new)
    return direction.reshape(row_width, col_width, blocks).transpose(2, 0, 1), left_new, right_new


def solution(mesh):
    placed = (
        P(None, "fsdp", "rep"),
        P(),
        P(("rep", "fsdp"), None),
        P(("rep", "fsdp"), None),
        P(("rep", "fsdp"), None),
        P(("rep", "fsdp"), None),
    )
    return jax.shard_map(
        per_device,
        mesh=mesh,
        in_specs=placed,
        out_specs=(P(None, "fsdp", "rep"), P(("rep", "fsdp"), None), P(("rep", "fsdp"), None)),
        check_vma=False,
    )
```
